32 devices in a mesh: blk: 16 (over z, y, x), head: 2 (over core).
Axes of the slice: x: 2, y: 2, z: 4, core: 2. Of those that a mesh axis runs over, the one named last changes fastest.
Arguments:
- query_rows: bfloat16 [4096, 2048], P(('blk', 'head')), may hold values from -30 to 30
- key_rows: bfloat16 [4096, 2048], P(('blk', 'head')), may hold values from -30 to 30
- value_rows: bfloat16 [4096, 2048], P(('blk', 'head')), may hold values from -6 to 6
- out_grad: bfloat16 [4096, 2048], P(('blk', 'head')), may hold values from -6 to 6
- doc_ids: int32 [4096], replicated, may hold values from 0 to 31, never falling along the last dimension, each value on 1 to 256 neighbouring positions
Outputs:
- attended: bfloat16 [4096, 2048], P(('blk', 'head'))
- query_grad: bfloat16 [4096, 2048], P(('blk', 'head'))
- key_grad: bfloat16 [4096, 2048], P(('blk', 'head'))
- value_grad: bfloat16 [4096, 2048], P(('blk', 'head'))
The draws below stay inside these ranges and needn't reach their ends.
Inputs may be any that keep to these rules, and one draw needn't show every extreme that they name: doc_ids never fall; each document holds 1 to 256 tokens, one exactly 256.
All inputs are finite; a program needn't handle non-finite values.
Results may differ from the reference program's by a relative error of at most 0.02.
Values may be sent and summed in bfloat16 or wider, within the bound.
No kernel may reach another device: no remote copies, remote signals or barrier semaphores. Data moves between devices by JAX's collectives and lax.ppermute only.
A program may use at most 64 MiB of HBM per device.

```python
import math
import jax
import jax.numpy as jnp
import numpy as np
from jax import lax

HEADS = 16
DH = 128
TOK_DEV = 128
LEN = 4096
DOC_MOST = 256
DOCS = 32


def draw_query_rows(key, part):
    key = jax.random.fold_in(key, 11)
    drawn = jnp.clip(jax.random.normal(key, (LEN, HEADS * DH), jnp.float32), -6.0, 6.0)
    return drawn.astype(jnp.bfloat16)


def draw_key_rows(key, part):
    key = jax.random.fold_in(key, 23)
    drawn = jnp.clip(jax.random.normal(key, (LEN, HEADS * DH), jnp.float32), -6.0, 6.0)
    return drawn.astype(jnp.bfloat16)


def block_scale(rng, shape, split, low, top_value):
    def one(position, blocks):
        steps = jax.random.uniform(jax.random.fold_in(jax.random.fold_in(rng, 6), position), (blocks,), jnp.float32, low / len(split), top_value / len(split))
        return jnp.repeat(jnp.exp(steps), shape[position] // blocks).reshape((-1,) + (1,) * (len(shape) - position - 1))

    level = one(*split[0])
    for cut in split[1:]:
        level = level * one(*cut)
    return level


def profile(count, total, reach, slope):
    portions = [(1 << 20) // math.isqrt(rank ** slope) + 1 for rank in range(2, count + 1)]
    rest, counts = total - reach - (count - 1), [1] * (count - 1)
    while rest > 0:
        movable = [i for i in range(count - 1) if counts[i] < reach]
        pool, left = sum([portions[i] for i in movable]), rest
        for i in movable:
            addition = min(reach - counts[i], max(1, left * portions[i] // pool), rest)
            counts[i] = counts[i] + addition
            rest = rest - addition
    return np.array([reach] + counts)


def uneven(own_key, amount, total, most, slope):
    if amount == 2:
        one = jax.random.randint(own_key, (), max(1, total - most), min(most, total - 1) + 1)
        return jnp.stack([one, total - one])
    tallies = jnp.asarray(profile(amount, total, most, slope), jnp.int32)
    pairs = (amount - 1) // 2
    donor, sink = tallies[1:1 + 2 * pairs:2], tallies[2:2 + 2 * pairs:2]
    room = jnp.minimum(donor - 1, most - sink)
    moved = jax.random.randint(jax.random.fold_in(own_key, 1), (pairs,), 0, 1 << 20) % (room + 1)
    tallies = tallies.at[1:1 + 2 * pairs:2].set(donor - moved).at[2:2 + 2 * pairs:2].set(sink + moved)
    return tallies[jax.random.permutation(jax.random.fold_in(own_key, 2), amount)]


def scatter_about(rng, shape, scale, limit, split=(), held_as=jnp.bfloat16):
    level = block_scale(rng, shape, split, -0.22, 0.18) if split else 1.0
    array = jax.random.normal(rng, shape, jnp.float32) * scale * level
    return jnp.minimum(jnp.maximum(array, -limit), limit).astype(held_as)


def setup_inputs(seed: int = 0) -> dict:
    seeds = jax.random.split(jax.random.key(seed), 6)
    return {
        "query_rows": draw_query_rows(jax.random.fold_in(seeds[5], 71), 0),
        "key_rows": draw_key_rows(jax.random.fold_in(seeds[5], 71), 0),
        "value_rows": scatter_about(seeds[2], (LEN, HEADS * DH), 1.0, 6.0, ((0, 32),)),
        "out_grad": scatter_about(seeds[3], (LEN, HEADS * DH), 1.0, 6.0, ((0, 32),)),
        "doc_ids": jnp.searchsorted(jnp.cumsum(uneven(seeds[4], DOCS, LEN, DOC_MOST, 2)), jnp.arange(LEN), side="right").astype(jnp.int32),
    }


def reference(query_rows, key_rows, value_rows, out_grad, doc_ids):
    score_scale = 1.0 / math.sqrt(DH)
    band = 5 * TOK_DEV
    margin = 2 * TOK_DEV

    def by_head(matrix):
        heads = matrix.reshape(LEN, HEADS, DH).transpose(1, 0, 2)
        return jnp.pad(heads, ((0, 0), (margin, margin), (0, 0)))

    def to_rows(blocks):
        return blocks.transpose(0, 2, 1, 3).reshape(LEN, HEADS * DH)
    query_pad = by_head(query_rows)
    key_pad = by_head(key_rows)
    value_pad = by_head(value_rows)
    grad_pad = by_head(out_grad)
    ids_pad = jnp.pad(doc_ids, (margin, margin), constant_values=-1)

    def forward_block(block_no):
        own_at = (block_no * TOK_DEV + margin).astype(jnp.int32)
        band_at = (block_no * TOK_DEV).astype(jnp.int32)
        query_own = lax.dynamic_slice_in_dim(query_pad, own_at, TOK_DEV, 1).astype(jnp.float32)
        grad_own = lax.dynamic_slice_in_dim(grad_pad, own_at, TOK_DEV, 1).astype(jnp.float32)
        key_band = lax.dynamic_slice_in_dim(key_pad, band_at, band, 1).astype(jnp.float32)
        value_band = lax.dynamic_slice_in_dim(value_pad, band_at, band, 1).astype(jnp.float32)
        same_doc = (lax.dynamic_slice_in_dim(ids_pad, own_at, TOK_DEV)[:, None] == lax.dynamic_slice_in_dim(ids_pad, band_at, band)[None, :])[None]
        scores = jnp.einsum('hqd,hkd->hqk', query_own, key_band) * score_scale
        scores = jnp.where(same_doc, scores, jnp.float32(-1e+30))
        row_top = lax.optimization_barrier(jnp.max(scores, axis=2, keepdims=True))
        log_total = row_top + jnp.log(lax.optimization_barrier(jnp.sum(jnp.exp(scores - row_top), axis=2, keepdims=True)))
        prob_tile = jnp.where(same_doc, jnp.exp(scores - log_total), jnp.float32(0.0))
        probs_low = prob_tile.astype(jnp.bfloat16)
        attended = jnp.einsum('hqk,hkd->hqd', probs_low.astype(jnp.float32), value_band).astype(jnp.bfloat16)
        row_delta = lax.optimization_barrier(jnp.sum(grad_own * attended.astype(jnp.float32), axis=2, keepdims=True))
        prob_grad = jnp.einsum('hqd,hkd->hqk', grad_own, value_band)
        score_low = (prob_tile * (prob_grad - row_delta)).astype(jnp.bfloat16)
        query_grad = (score_scale * jnp.einsum('hqk,hkd->hqd', score_low.astype(jnp.float32), key_band)).astype(jnp.bfloat16)
        return (attended, query_grad, log_total[:, :, 0], row_delta[:, :, 0])
    blocks = jnp.arange(LEN // TOK_DEV, dtype=jnp.int32)
    attended, query_grad, log_total, row_delta = lax.map(forward_block, blocks)
    lse_pad = jnp.pad(log_total.transpose(1, 0, 2).reshape(HEADS, LEN), ((0, 0), (margin, margin)))
    delta_pad = jnp.pad(row_delta.transpose(1, 0, 2).reshape(HEADS, LEN), ((0, 0), (margin, margin)))

    def key_block(block_no):
        own_at = (block_no * TOK_DEV + margin).astype(jnp.int32)
        band_at = (block_no * TOK_DEV).astype(jnp.int32)
        key_own = lax.dynamic_slice_in_dim(key_pad, own_at, TOK_DEV, 1).astype(jnp.float32)
        value_own = lax.dynamic_slice_in_dim(value_pad, own_at, TOK_DEV, 1).astype(jnp.float32)
        query_band = lax.dynamic_slice_in_dim(query_pad, band_at, band, 1).astype(jnp.float32)
        grad_band = lax.dynamic_slice_in_dim(grad_pad, band_at, band, 1).astype(jnp.float32)
        lse_band = lax.dynamic_slice_in_dim(lse_pad, band_at, band, 1)
        delta_band = lax.dynamic_slice_in_dim(delta_pad, band_at, band, 1)
        same_doc = (lax.dynamic_slice_in_dim(ids_pad, band_at, band)[:, None] == lax.dynamic_slice_in_dim(ids_pad, own_at, TOK_DEV)[None, :])[None]
        scores = jnp.einsum('hqd,hkd->hqk', query_band, key_own) * score_scale
        scores = jnp.where(same_doc, scores, jnp.float32(-1e+30))
        prob_tile = jnp.where(same_doc, jnp.exp(scores - lse_band[:, :, None]), jnp.float32(0.0))
        probs_low = prob_tile.astype(jnp.bfloat16)
        value_grad = jnp.einsum('hqk,hqd->hkd', probs_low.astype(jnp.float32), grad_band).astype(jnp.bfloat16)
        prob_grad = jnp.einsum('hqd,hkd->hqk', grad_band, value_own)
        score_low = (prob_tile * (prob_grad - delta_band[:, :, None])).astype(jnp.bfloat16)
        key_grad = (score_scale * jnp.einsum('hqk,hqd->hkd', score_low.astype(jnp.float32), query_band)).astype(jnp.bfloat16)
        return (key_grad, value_grad)
    key_grad, value_grad = lax.map(key_block, blocks)
    return (to_rows(attended), to_rows(query_grad), to_rows(key_grad), to_rows(value_grad))
```

```python
import functools
import math

import jax
import jax.numpy as jnp
from jax import lax
from jax.experimental import pallas as pl
from jax.experimental.pallas import tpu as pltpu
from jax.sharding import PartitionSpec as P

DH = 128
DOC_MOST = 256
MASKED = -1e30
CHUNKS = (1, 2, 2, 2, 1)
SCALE = 1.0 / math.sqrt(DH)
VMEM = 60 * 1024 * 1024


def dot_nt(a, b):
    return lax.dot_general(a, b, (((1,), (1,)), ((), ())), preferred_element_type=jnp.float32)


def dot_tn(a, b):
    return lax.dot_general(a, b, (((0,), (0,)), ((), ())), preferred_element_type=jnp.float32)


def dot_nn(a, b):
    return lax.dot_general(a, b, (((1,), (0,)), ((), ())), preferred_element_type=jnp.float32)


def tile_probs(keys, queries, key_ids, query_ids):
    scores = dot_nt(keys, queries) * (SCALE * math.log2(math.e))
    scores = jnp.where(key_ids == query_ids, scores, jnp.float32(MASKED))
    top = jnp.max(scores, axis=0, keepdims=True)
    weights = jnp.exp2(scores - top)
    return weights * (1.0 / jnp.sum(weights, axis=0, keepdims=True))


def attend(probs_low, values, grads):
    attended = dot_tn(values, probs_low).astype(jnp.bfloat16)
    delta = jnp.sum(
        attended.astype(jnp.float32) * grads.T.astype(jnp.float32), axis=0, keepdims=True
    )
    return attended, delta


def attention_kernel(heads, own_ref, near_ref, far_ref, row_ids_ref, col_ids_ref, keep_ref, send_ref):
    rows = 2 * own_ref.shape[2]
    half = own_ref.shape[2]
    own_cols = col_ids_ref[0:rows, :]
    own_lane = row_ids_ref[:, 0:rows]

    def rows_of(ref, member, h):
        lanes = slice(h * DH, (h + 1) * DH)
        return jnp.concatenate([ref[0, member, :, lanes], ref[1, member, :, lanes]], axis=0)

    for h in range(heads):
        q_own, k_own, v_own, g_own = (rows_of(own_ref, m, h) for m in range(4))
        q_near, k_near, v_near, g_near = (rows_of(near_ref, m, h) for m in range(4))
        q_far, k_far, v_far, g_far = (rows_of(far_ref, m, h) for m in range(4))
        keys = jnp.concatenate([k_own, k_near, k_far], axis=0)
        values = jnp.concatenate([v_own, v_near, v_far], axis=0)
        probs = tile_probs(keys, q_own, col_ids_ref[...], own_lane)
        low = probs.astype(jnp.bfloat16)
        attended, delta = attend(low, values, g_own)
        score_grad = (probs * (dot_nt(values, g_own) - delta)).astype(jnp.bfloat16)
        query_grad = dot_tn(keys, score_grad) * SCALE
        key_grad = dot_nn(score_grad[0:rows], q_own)
        value_grad = dot_nn(low[0:rows], g_own)
        for side, (q_side, k_side, v_side, g_side) in enumerate(
            ((q_near, k_near, v_near, g_near), (q_far, k_far, v_far, g_far))
        ):
            at = slice((side + 1) * rows, (side + 2) * rows)
            side_cols = jnp.concatenate([own_cols, col_ids_ref[at, :]], axis=0)
            probs = tile_probs(
                jnp.concatenate([k_own, k_side], axis=0), q_side, side_cols, row_ids_ref[:, at]
            )
            low = probs.astype(jnp.bfloat16)
            _, delta = attend(low, jnp.concatenate([v_own, v_side], axis=0), g_side)
            score_grad = (probs[0:rows] * (dot_nt(v_own, g_side) - delta)).astype(jnp.bfloat16)
            key_grad = key_grad + dot_nn(score_grad, q_side)
            value_grad = value_grad + dot_nn(low[0:rows], g_side)
        results = (
            attended.astype(jnp.float32).T.astype(jnp.bfloat16),
            query_grad.T.astype(jnp.bfloat16),
            (key_grad * SCALE).astype(jnp.bfloat16),
            value_grad.astype(jnp.bfloat16),
        )
        lanes = slice(h * DH, (h + 1) * DH)
        for m, result in enumerate(results):
            keep_ref[m, :, lanes] = result[0:half]
            send_ref[m, :, lanes] = result[half:rows]


def attention(own, near, far, row_ids, col_ids):
    _, members, half, width = own.shape
    heads = width // DH
    whole = pl.BlockSpec(memory_space=pltpu.VMEM)
    out = jax.ShapeDtypeStruct((members, half, width), jnp.bfloat16)
    rows = 2 * half
    flops = heads * 2 * DH * rows * rows * (5 * 3 + 2 * (2 + 2 + 1 + 2))
    return pl.pallas_call(
        functools.partial(attention_kernel, heads),
        out_shape=(out, out),
        in_specs=[whole] * 5,
        out_specs=(whole, whole),
        compiler_params=pltpu.CompilerParams(vmem_limit_bytes=VMEM),
        cost_estimate=pl.CostEstimate(
            flops=flops, bytes_accessed=4 * own.size * 2, transcendentals=heads * 7 * rows * rows
        ),
    )(own, near, far, row_ids, col_ids)


def pack_kernel(chunks, q_ref, k_ref, v_ref, g_ref, *outs):
    mine, other = outs[: len(chunks)], outs[len(chunks) :]
    head_half = q_ref.shape[1] // 2
    core = lax.axis_index("head")
    for m, ref in enumerate((q_ref, k_ref, v_ref, g_ref)):
        at = 0
        for j, heads in enumerate(chunks):
            width = heads * DH
            for group, place in ((mine, core), (other, 1 - core)):
                first = pl.multiple_of(place * head_half + at, DH)
                group[j][m] = ref[:, pl.ds(first, width)]
            at += width


def pack(arrays, chunks):
    rows, width = arrays[0].shape
    steps = 2
    block = rows // steps
    shapes = [jax.ShapeDtypeStruct((4, rows, heads * DH), jnp.bfloat16) for heads in chunks] * 2
    got = pl.pallas_call(
        functools.partial(pack_kernel, chunks),
        grid=(steps,),
        out_shape=shapes,
        in_specs=[pl.BlockSpec((block, width), lambda i: (i, 0))] * 4,
        out_specs=[pl.BlockSpec((4, block, s.shape[2]), lambda i: (0, i, 0)) for s in shapes],
        compiler_params=pltpu.CompilerParams(vmem_limit_bytes=VMEM),
    )(*arrays)
    return got[: len(chunks)], got[len(chunks) :]


def unpack_kernel(chunks, *refs):
    count = len(chunks)
    kept, received, outs = refs[:count], refs[count : 2 * count], refs[2 * count :]
    head_half = outs[0].shape[1] // 2
    core = lax.axis_index("head")
    for m, ref in enumerate(outs):
        at = 0
        for j, heads in enumerate(chunks):
            width = heads * DH
            for group, place in ((kept, core), (received, 1 - core)):
                first = pl.multiple_of(place * head_half + at, DH)
                ref[:, pl.ds(first, width)] = group[j][m]
            at += width


def unpack(kept, received, chunks, width):
    rows = kept[0].shape[1]
    steps = 2
    block = rows // steps
    return pl.pallas_call(
        functools.partial(unpack_kernel, chunks),
        grid=(steps,),
        out_shape=[jax.ShapeDtypeStruct((rows, width), jnp.bfloat16)] * 4,
        in_specs=[
            pl.BlockSpec((4, block, t.shape[2]), lambda i: (0, i, 0)) for t in (*kept, *received)
        ],
        out_specs=[pl.BlockSpec((block, width), lambda i: (i, 0))] * 4,
        compiler_params=pltpu.CompilerParams(vmem_limit_bytes=VMEM),
    )(*kept, *received)


def neighbour_ids(doc_ids, rows):
    positions = lax.axis_size("blk")
    here, core = lax.axis_index("blk"), lax.axis_index("head")
    away = 1 - 2 * (here % 2)
    table = doc_ids.reshape(-1, rows)
    picked = []
    for place in (here, here + away, here - away):
        inside = (place >= 0) & (place < positions)
        held = jnp.clip(place, 0, positions - 1)
        for which in (core, 1 - core):
            row = lax.dynamic_index_in_dim(table, 2 * held + which, 0, keepdims=False)
            picked.append(jnp.where(inside, row, -1))
    return jnp.concatenate(picked)


def body(query_rows, key_rows, value_rows, out_grad, doc_ids):
    positions = lax.axis_size("blk")
    rows, width = query_rows.shape
    chunks = CHUNKS
    swap = [(0, 1), (1, 0)]
    pairs = [(i, i ^ 1) for i in range(positions)]
    onward = [(i, i + 2) for i in range(0, positions - 2, 2)]
    onward += [(i, i - 2) for i in range(3, positions, 2)]
    ids = neighbour_ids(doc_ids, rows)
    row_ids, col_ids = ids[None, :], ids[:, None]

    mine, other = pack((query_rows, key_rows, value_rows, out_grad), chunks)
    kept, received = [], []
    for own, away in zip(mine, other):
        own = jnp.stack([own, lax.ppermute(away, "head", swap)])
        near = lax.ppermute(own, "blk", pairs)
        far = lax.ppermute(near, "blk", onward)
        keep, send = attention(own, near, far, row_ids, col_ids)
        kept.append(keep)
        received.append(lax.ppermute(send, "head", swap))
    return tuple(unpack(kept, received, chunks, width))


def solution(mesh):
    placed = P(("blk", "head"), None)
    return jax.shard_map(
        body,
        mesh=mesh,
        in_specs=(placed, placed, placed, placed, P()),
        out_specs=(placed,) * 4,
        check_vma=False,
    )
```

```python
import functools
import math

import jax
import jax.numpy as jnp
from jax import lax
from jax.experimental import pallas as pl
from jax.experimental.pallas import tpu as pltpu
from jax.sharding import PartitionSpec as P

DH = 128
DOC_MOST = 256
MASKED = -1e30
GROUP = 4
SCALE = 1.0 / math.sqrt(DH)
VMEM = 60 * 1024 * 1024
WHOLE = pl.BlockSpec(memory_space=pltpu.VMEM)


def dot_nt(a, b):
    return lax.dot_general(a, b, (((1,), (1,)), ((), ())), preferred_element_type=jnp.float32)


def dot_tn(a, b):
    return lax.dot_general(a, b, (((0,), (0,)), ((), ())), preferred_element_type=jnp.float32)


def dot_nn(a, b):
    return lax.dot_general(a, b, (((1,), (0,)), ((), ())), preferred_element_type=jnp.float32)


def stack_rows(*blocks):
    return jnp.concatenate(blocks, axis=0)


def tile_probs(keys, queries, key_ids, query_ids):
    scores = dot_nt(keys, queries) * (SCALE * math.log2(math.e))
    scores = jnp.where(key_ids == query_ids, scores, jnp.float32(MASKED))
    top = jnp.max(scores, axis=0, keepdims=True)
    weights = jnp.exp2(scores - top)
    return weights * (1.0 / jnp.sum(weights, axis=0, keepdims=True))


def attend(probs_low, values, grads):
    attended = dot_tn(values, probs_low).astype(jnp.bfloat16)
    delta = jnp.sum(
        attended.astype(jnp.float32) * grads.T.astype(jnp.float32), axis=0, keepdims=True
    )
    return attended, delta


def query_block(queries, grads, keys, values, key_ids, query_ids):
    probs = tile_probs(keys, queries, key_ids, query_ids)
    low = probs.astype(jnp.bfloat16)
    attended, delta = attend(low, values, grads)
    score_grad = (probs * (dot_nt(values, grads) - delta)).astype(jnp.bfloat16)
    query_grad = (dot_tn(keys, score_grad) * SCALE).T.astype(jnp.bfloat16)
    attended = attended.astype(jnp.float32).T.astype(jnp.bfloat16)
    return attended, query_grad, score_grad, low


def interior_kernel(edge, ext_ref, row_ids_ref, col_ids_ref, done_ref, part_ref):
    rows = ext_ref.shape[1]
    blocks = rows // edge
    part_ref[...] = jnp.zeros_like(part_ref)
    for b in range(1, blocks - 1):
        at = slice(b * edge, (b + 1) * edge)
        band = slice((b - 1) * edge, (b + 2) * edge)
        ids = slice(b * edge, (b + 3) * edge)
        queries, grads = ext_ref[0, at], ext_ref[3, at]
        attended, query_grad, score_grad, low = query_block(
            queries,
            grads,
            ext_ref[1, band],
            ext_ref[2, band],
            col_ids_ref[ids, :],
            row_ids_ref[:, (b + 1) * edge : (b + 2) * edge],
        )
        done_ref[0, (b - 1) * edge : b * edge] = attended
        done_ref[1, (b - 1) * edge : b * edge] = query_grad
        part_ref[0, band] += dot_nn(score_grad, queries)
        part_ref[1, band] += dot_nn(low, grads)


def edge_kernel(edge, ext_ref, even_ref, odd_ref, done_ref, part_ref, row_ids_ref, col_ids_ref, *refs):
    outs, (result, acc_ref) = refs[:-2], refs[-2:]
    rows = ext_ref.shape[1]
    blocks = rows // edge
    position, core = lax.axis_index("blk"), lax.axis_index("head")
    place, parity = position % GROUP, (position // GROUP) % 2
    acc_ref[...] = part_ref[...]
    for m in range(2):
        result[m, edge : rows - edge] = done_ref[m]
    for side in range(2):
        from_even = parity == (1 - side)
        q_halo, k_halo, v_halo, g_halo = (
            jnp.where(from_even, even_ref[m], odd_ref[m]) for m in range(4)
        )
        own = slice(0, edge) if side == 0 else slice(rows - edge, rows)
        own_ids = slice(edge, 2 * edge) if side == 0 else slice(rows, rows + edge)
        halo_ids = slice(0, edge) if side == 0 else slice(rows + edge, rows + 2 * edge)
        wide = slice(0, 2 * edge) if side == 0 else slice(rows - 2 * edge, rows)
        wide_ids = slice(edge, 3 * edge) if side == 0 else slice(rows - edge, rows + edge)
        queries, grads = ext_ref[0, own], ext_ref[3, own]
        attended, query_grad, score_grad, low = query_block(
            queries,
            grads,
            stack_rows(ext_ref[1, wide], k_halo),
            stack_rows(ext_ref[2, wide], v_halo),
            stack_rows(col_ids_ref[wide_ids, :], col_ids_ref[halo_ids, :]),
            row_ids_ref[:, own_ids],
        )
        result[0, own] = attended
        result[1, own] = query_grad
        acc_ref[0, wide] += dot_nn(score_grad[: 2 * edge], queries)
        acc_ref[1, wide] += dot_nn(low[: 2 * edge], grads)
        keys, values = ext_ref[1, own], ext_ref[2, own]
        probs = tile_probs(
            stack_rows(keys, k_halo),
            q_halo,
            stack_rows(col_ids_ref[own_ids, :], col_ids_ref[halo_ids, :]),
            row_ids_ref[:, halo_ids],
        )
        low = probs.astype(jnp.bfloat16)
        _, delta = attend(low, stack_rows(values, v_halo), g_halo)
        score_grad = (probs[:edge] * (dot_nt(values, g_halo) - delta)).astype(jnp.bfloat16)
        acc_ref[0, own] += dot_nn(score_grad, q_halo)
        acc_ref[1, own] += dot_nn(low[:edge], g_halo)
    result[2] = (acc_ref[0] * SCALE).astype(jnp.bfloat16)
    result[3] = acc_ref[1].astype(jnp.bfloat16)
    half = outs[0].shape[2]
    for s, out in enumerate(outs):
        chip = place ^ s
        for piece in range(2):
            first = pl.multiple_of((chip * 2 + (core ^ piece)) * half, half)
            for m in range(4):
                out[piece, m] = result[m, pl.ds(first, half), :]


def call(kernel, out_shape, *args, scratch=(), flops=0, exps=0):
    return pl.pallas_call(
        kernel,
        out_shape=out_shape,
        in_specs=[WHOLE] * len(args),
        out_specs=jax.tree.map(lambda _: WHOLE, out_shape),
        scratch_shapes=scratch,
        compiler_params=pltpu.CompilerParams(vmem_limit_bytes=VMEM),
        cost_estimate=pl.CostEstimate(
            flops=flops, bytes_accessed=sum(a.size * 2 for a in args), transcendentals=exps
        ),
    )(*args)


def shape(*dims, dtype=jnp.bfloat16):
    return jax.ShapeDtypeStruct(dims, dtype)


def pack_kernel(q_ref, k_ref, v_ref, g_ref, *outs):
    chunks = len(outs) // 2
    head_half = q_ref.shape[1] // 2
    core, place = lax.axis_index("head"), lax.axis_index("blk") % GROUP
    for which in range(2):
        for s in range(GROUP):
            base = (core ^ which) * head_half + (place ^ s) * chunks * DH
            for j in range(chunks):
                first = pl.multiple_of(base + j * DH, DH)
                for m, ref in enumerate((q_ref, k_ref, v_ref, g_ref)):
                    outs[which * chunks + j][s, m] = ref[:, pl.ds(first, DH)]


def pack(arrays, chunks):
    rows, width = arrays[0].shape
    steps = 2
    block = rows // steps
    got = pl.pallas_call(
        pack_kernel,
        grid=(steps,),
        out_shape=[shape(GROUP, 4, rows, DH)] * (2 * chunks),
        in_specs=[pl.BlockSpec((block, width), lambda i: (i, 0))] * 4,
        out_specs=[pl.BlockSpec((GROUP, 4, block, DH), lambda i: (0, 0, i, 0))] * (2 * chunks),
        compiler_params=pltpu.CompilerParams(vmem_limit_bytes=VMEM),
    )(*arrays)
    return got[:chunks], got[chunks:]


def join_kernel(mine_ref, received_ref, *outs):
    for s, out in enumerate(outs):
        out[0] = mine_ref[s]
        out[1] = received_ref[s]


def gather_kernel(*refs):
    slots, (ext, to_even, to_odd) = refs[:GROUP], refs[GROUP:]
    half, edge = slots[0].shape[2], to_even.shape[1]
    position, core = lax.axis_index("blk"), lax.axis_index("head")
    place, parity = position % GROUP, (position // GROUP) % 2
    for s, slot in enumerate(slots):
        for piece in range(2):
            first = pl.multiple_of(((place ^ s) * 2 + (core ^ piece)) * half, half)
            for m in range(4):
                ext[m, pl.ds(first, half), :] = slot[piece, m]
    rows = ext.shape[1]
    first = pl.multiple_of((rows - edge) * (1 - parity), edge)
    to_even[...] = ext[:, pl.ds(first, edge), :]
    first = pl.multiple_of((rows - edge) * parity, edge)
    to_odd[...] = ext[:, pl.ds(first, edge), :]


def split_kernel(*refs):
    slots, out = refs[:-1], refs[-1]
    for s, slot in enumerate(slots):
        out[s] = slot[1]


def unpack_kernel(chunks, *refs):
    kept, received, outs = refs[: chunks * GROUP], refs[chunks * GROUP : -4], refs[-4:]
    head_half = outs[0].shape[1] // 2
    core, place = lax.axis_index("head"), lax.axis_index("blk") % GROUP
    for s in range(GROUP):
        for j in range(chunks):
            for which in range(2):
                base = (core ^ which) * head_half + (place ^ s) * chunks * DH
                first = pl.multiple_of(base + j * DH, DH)
                for m, out in enumerate(outs):
                    block = kept[j * GROUP + s][0, m] if which == 0 else received[j][s, m]
                    out[:, pl.ds(first, DH)] = block


def unpack(kept, received, width):
    chunks = len(received)
    rows = received[0].shape[2]
    steps = 2
    block = rows // steps
    flat = [slot for chunk in kept for slot in chunk]
    return pl.pallas_call(
        functools.partial(unpack_kernel, chunks),
        grid=(steps,),
        out_shape=[shape(rows, width)] * 4,
        in_specs=[pl.BlockSpec((1, 4, block, DH), lambda i: (0, 0, i, 0))] * len(flat)
        + [pl.BlockSpec((GROUP, 4, block, DH), lambda i: (0, 0, i, 0))] * chunks,
        out_specs=[pl.BlockSpec((block, width), lambda i: (i, 0))] * 4,
        compiler_params=pltpu.CompilerParams(vmem_limit_bytes=VMEM),
    )(*flat, *received)


def body(query_rows, key_rows, value_rows, out_grad, doc_ids):
    positions = lax.axis_size("blk")
    half, width = query_rows.shape
    heads = width // DH
    chunks = heads // (2 * GROUP)
    edge = 2 * half
    rows = GROUP * edge
    swap = [(0, 1), (1, 0)]
    hops = [[(i, i ^ s) for i in range(positions)] for s in range(GROUP)]
    planes = positions // GROUP

    def plane_pairs(first):
        route = []
        for low in range(first, planes - 1, 2):
            for i in range(GROUP):
                here, there = low * GROUP + i, (low + 1) * GROUP + i
                route += [(here, there), (there, here)]
        return route

    plane = lax.axis_index("blk") // GROUP
    padded = jnp.pad(doc_ids, (edge, edge), constant_values=-1)
    ids = lax.dynamic_slice_in_dim(padded, plane * rows, rows + 2 * edge, 0)
    row_ids, col_ids = ids[None, :], ids[:, None]

    def exchange(slots):
        return [slots[0]] + [lax.ppermute(slots[s], "blk", hops[s]) for s in range(1, GROUP)]

    mine, other = pack((query_rows, key_rows, value_rows, out_grad), chunks)
    slot = shape(2, 4, half, DH)
    kept, received = [], []
    for j in range(chunks):
        theirs = lax.ppermute(other[j], "head", swap)
        slots = exchange(call(join_kernel, [slot] * GROUP, mine[j], theirs))
        ext, to_even, to_odd = call(
            gather_kernel, [shape(4, rows, DH), shape(4, edge, DH), shape(4, edge, DH)], *slots
        )
        even = lax.ppermute(to_even, "blk", plane_pairs(0))
        odd = lax.ppermute(to_odd, "blk", plane_pairs(1))
        unit = 2 * DH * edge * edge
        done, part = call(
            functools.partial(interior_kernel, edge),
            [shape(2, rows - 2 * edge, DH), shape(2, rows, DH, dtype=jnp.float32)],
            ext,
            row_ids,
            col_ids,
            flops=unit * 36,
            exps=6 * edge * edge,
        )
        back = call(
            functools.partial(edge_kernel, edge),
            [slot] * GROUP,
            ext,
            even,
            odd,
            done,
            part,
            row_ids,
            col_ids,
            scratch=[
                pltpu.VMEM((4, rows, DH), jnp.bfloat16),
                pltpu.VMEM((2, rows, DH), jnp.float32),
            ],
            flops=unit * 50,
            exps=10 * edge * edge,
        )
        back = exchange(back)
        kept.append(back)
        away = call(split_kernel, shape(GROUP, 4, half, DH), *back)
        received.append(lax.ppermute(away, "head", swap))
    return tuple(unpack(kept, received, width))


def solution(mesh):
    placed = P(("blk", "head"), None)
    return jax.shard_map(
        body,
        mesh=mesh,
        in_specs=(placed, placed, placed, placed, P()),
        out_specs=(placed,) * 4,
        check_vma=False,
    )
```

```python
import functools
import math

import jax
import jax.numpy as jnp
from jax import lax
from jax.experimental import pallas as pl
from jax.experimental.pallas import tpu as pltpu
from jax.sharding import PartitionSpec as P

DH = 128
DOC_MOST = 256
MASKED = -1e30
GROUP = 4
WHOLE_IN = (False, False)
WHOLE_OUT = (False, False)
SCALE = 1.0 / math.sqrt(DH)
VMEM = 12 * 1024 * 1024
PACK_VMEM = 61 * 1024 * 1024 + 512 * 1024
WHOLE = pl.BlockSpec(memory_space=pltpu.VMEM)


def dot_nt(a, b):
    return lax.dot_general(a, b, (((1,), (1,)), ((), ())), preferred_element_type=jnp.float32)


def dot_tn(a, b):
    return lax.dot_general(a, b, (((0,), (0,)), ((), ())), preferred_element_type=jnp.float32)


def dot_nn(a, b):
    return lax.dot_general(a, b, (((1,), (0,)), ((), ())), preferred_element_type=jnp.float32)


def self_attention(queries, keys, values, grads, same):
    scores = dot_nt(keys, queries) * (SCALE * math.log2(math.e))
    scores = jnp.where(same, scores, jnp.float32(MASKED))
    top = jnp.max(scores, axis=0, keepdims=True)
    weights = jnp.exp2(scores - top)
    probs = weights * (1.0 / jnp.sum(weights, axis=0, keepdims=True))
    low = probs.astype(jnp.bfloat16)
    attended = dot_tn(values, low).astype(jnp.bfloat16).astype(jnp.float32)
    delta = jnp.sum(attended * grads.T.astype(jnp.float32), axis=0, keepdims=True)
    score_grad = (probs * (dot_nt(values, grads) - delta)).astype(jnp.bfloat16)
    query_grad = (dot_tn(keys, score_grad) * SCALE).T
    key_grad = dot_nn(score_grad, queries) * SCALE
    value_grad = dot_nn(low, grads)
    return attended.T, query_grad, key_grad, value_grad


def crossing(low_ids, high_ids, first, last):
    return low_ids == first, high_ids == last


def boundary_attention(low_rows, high_rows, ids_low, ids_high):
    (low_col, low_lane), (high_col, high_lane) = ids_low, ids_high
    first, last = high_col[0:1, :], low_col[-1:, :]
    from_low, from_high = low_col == first, high_col == last
    lane_low = low_lane == first
    lane_high = high_lane == last
    member_col = (from_low | from_high).astype(jnp.int32)
    member_lane = (lane_low | lane_high).astype(jnp.int32)
    chosen = [
        jnp.where(from_low, a.astype(jnp.float32), b.astype(jnp.float32)).astype(jnp.bfloat16)
        for a, b in zip(low_rows, high_rows)
    ]
    return self_attention(*chosen, member_col == member_lane), from_low, from_high


def interior_kernel(edge, ext_ref, row_ids_ref, col_ids_ref, res_ref):
    tiles = ext_ref.shape[1] // edge

    def rows_of(t):
        return [ext_ref[m, t * edge : (t + 1) * edge] for m in range(4)]

    def ids_of(t):
        at = slice((t + 1) * edge, (t + 2) * edge)
        return col_ids_ref[at, :], row_ids_ref[:, at]

    def put(t, chosen, results):
        at = slice(t * edge, (t + 1) * edge)
        for m, result in enumerate(results):
            if chosen is not None:
                result = jnp.where(chosen, result, res_ref[m, at].astype(jnp.float32))
            res_ref[m, at] = result.astype(jnp.bfloat16)

    for t in range(tiles):
        col, lane = ids_of(t)
        put(t, None, self_attention(*rows_of(t), col == lane))
        if t > 0:
            results, from_low, from_high = boundary_attention(
                rows_of(t - 1), rows_of(t), ids_of(t - 1), ids_of(t)
            )
            put(t - 1, from_low, results)
            put(t, from_high, results)


def edge_kernel(edge, whole, ext_ref, even_ref, odd_ref, res_ref, row_ids_ref, col_ids_ref, *refs):
    outs, result_ref = refs[:-1], refs[-1]
    rows = ext_ref.shape[1]
    position, core = lax.axis_index("blk"), lax.axis_index("head")
    place, parity = position % GROUP, (position // GROUP) % 2
    result_ref[...] = res_ref[...]

    def ids_at(first):
        return col_ids_ref[first : first + edge, :], row_ids_ref[:, first : first + edge]

    for side in range(2):
        from_even = parity == (1 - side)
        halo = [jnp.where(from_even, even_ref[m], odd_ref[m]) for m in range(4)]
        own = slice(0, edge) if side == 0 else slice(rows - edge, rows)
        mine = [ext_ref[m, own] for m in range(4)]
        if side == 0:
            results, _, chosen = boundary_attention(halo, mine, ids_at(0), ids_at(edge))
        else:
            results, chosen, _ = boundary_attention(mine, halo, ids_at(rows), ids_at(rows + edge))
        for m, result in enumerate(results):
            result = jnp.where(chosen, result, result_ref[m, own].astype(jnp.float32))
            result_ref[m, own] = result.astype(jnp.bfloat16)
    half = edge // 2
    if whole:
        for i in range(2 * GROUP):
            outs[0][i] = result_ref[:, i * half : (i + 1) * half]
        return
    for s in range(GROUP):
        for piece in range(2):
            first = pl.multiple_of(((place ^ s) * 2 + (core ^ piece)) * half, half)
            outs[s][piece] = result_ref[:, pl.ds(first, half), :]


def shape(*dims, dtype=jnp.bfloat16):
    return jax.ShapeDtypeStruct(dims, dtype)


def call(kernel, out_shape, *args, scratch=(), flops=0, exps=0):
    return pl.pallas_call(
        kernel,
        out_shape=out_shape,
        in_specs=[WHOLE] * len(args),
        out_specs=jax.tree.map(lambda _: WHOLE, out_shape),
        scratch_shapes=scratch,
        compiler_params=pltpu.CompilerParams(vmem_limit_bytes=VMEM),
        cost_estimate=pl.CostEstimate(flops=1, bytes_accessed=1, transcendentals=0),
    )(*args)


def pack_kernel(wholes, *refs):
    ins, outs = refs[:4], list(refs[4:])
    width = ins[0].shape[1]
    chunks = len(wholes)
    core, place = lax.axis_index("head"), lax.axis_index("blk") % GROUP
    for j, whole in enumerate(wholes):
        if whole:
            out = outs.pop(0)
            for i in range(2 * GROUP):
                first = (i % 2) * (width // 2) + ((i // 2) * chunks + j) * DH
                for m, ref in enumerate(ins):
                    out[i, m] = ref[:, first : first + DH]
            continue
        for which in range(2):
            out = outs.pop(0)
            for s in range(GROUP):
                base = (core ^ which) * (width // 2) + ((place ^ s) * chunks + j) * DH
                first = pl.multiple_of(base, DH)
                for m, ref in enumerate(ins):
                    out[s, m] = ref[:, pl.ds(first, DH)]


def pack(arrays, wholes):
    rows, width = arrays[0].shape
    steps = 2
    block = rows // steps
    sizes = []
    for whole in wholes:
        sizes += [2 * GROUP] if whole else [GROUP, GROUP]
    got = list(
        pl.pallas_call(
            functools.partial(pack_kernel, wholes),
            grid=(steps,),
            out_shape=[shape(n, 4, rows, DH) for n in sizes],
            in_specs=[pl.BlockSpec((block, width), lambda i: (i, 0))] * 4,
            out_specs=[pl.BlockSpec((n, 4, block, DH), lambda i: (0, 0, i, 0)) for n in sizes],
            compiler_params=pltpu.CompilerParams(vmem_limit_bytes=PACK_VMEM),
        )(*arrays)
    )
    return [[got.pop(0) for _ in range(1 if whole else 2)] for whole in wholes]


def join_kernel(mine_ref, received_ref, *outs):
    for s, out in enumerate(outs):
        out[0] = mine_ref[s]
        out[1] = received_ref[s]


def gather_kernel(whole, *refs):
    slots, (ext, to_even, to_odd) = refs[:-3], refs[-3:]
    edge = to_even.shape[1]
    half = edge // 2
    position, core = lax.axis_index("blk"), lax.axis_index("head")
    place, parity = position % GROUP, (position // GROUP) % 2
    for i in range(2 * GROUP if whole else 0):
        ext[:, i * half : (i + 1) * half] = slots[0][i]
    for s in range(0 if whole else GROUP):
        for piece in range(2):
            first = pl.multiple_of(((place ^ s) * 2 + (core ^ piece)) * half, half)
            ext[:, pl.ds(first, half), :] = slots[s][piece]
    rows = ext.shape[1]
    first = pl.multiple_of((rows - edge) * (1 - parity), edge)
    to_even[...] = ext[:, pl.ds(first, edge), :]
    first = pl.multiple_of((rows - edge) * parity, edge)
    to_odd[...] = ext[:, pl.ds(first, edge), :]


def split_kernel(*refs):
    slots, out = refs[:-1], refs[-1]
    for s, slot in enumerate(slots):
        out[s] = slot[1]


def unpack_kernel(wholes, *refs):
    ins, outs = list(refs[:-4]), refs[-4:]
    width = outs[0].shape[1]
    chunks = len(wholes)
    core, place = lax.axis_index("head"), lax.axis_index("blk") % GROUP
    for j, whole in enumerate(wholes):
        if whole:
            block = ins.pop(0)
            for i in range(2 * GROUP):
                first = (i % 2) * (width // 2) + ((i // 2) * chunks + j) * DH
                for m, out in enumerate(outs):
                    out[:, first : first + DH] = block[i, m]
            continue
        slots = [ins.pop(0) for _ in range(GROUP)]
        received = ins.pop(0)
        for s in range(GROUP):
            for which in range(2):
                base = (core ^ which) * (width // 2) + ((place ^ s) * chunks + j) * DH
                first = pl.multiple_of(base, DH)
                for m, out in enumerate(outs):
                    out[:, pl.ds(first, DH)] = slots[s][0, m] if which == 0 else received[s, m]


def unpack(chunks, wholes, rows, width):
    blocks = [block for chunk in chunks for block in chunk]
    return call(functools.partial(unpack_kernel, wholes), [shape(rows, width)] * 4, *blocks)


def body(query_rows, key_rows, value_rows, out_grad, doc_ids):
    positions = lax.axis_size("blk")
    half, width = query_rows.shape
    heads = width // DH
    chunks = heads // (2 * GROUP)
    edge = 2 * half
    rows = GROUP * edge
    assert edge >= DOC_MOST and positions % GROUP == 0 and chunks == len(WHOLE_IN)
    swap = [(0, 1), (1, 0)]
    planes = positions // GROUP

    def plane_pairs(first):
        route = []
        for low in range(first, planes - 1, 2):
            for i in range(GROUP):
                here, there = low * GROUP + i, (low + 1) * GROUP + i
                route += [(here, there), (there, here)]
        return route

    def hop(block, s):
        return lax.ppermute(block, "blk", [(i, i ^ s) for i in range(positions)]) if s else block

    def all_to_all(block):
        size = 2 * GROUP
        groups = [[p * size + i for i in range(size)] for p in range(planes)]
        return lax.all_to_all(
            block, ("blk", "head"), split_axis=0, concat_axis=0, axis_index_groups=groups
        )

    plane = lax.axis_index("blk") // GROUP
    padded = jnp.pad(doc_ids, (edge, edge), constant_values=-1)
    ids = lax.dynamic_slice_in_dim(padded, plane * rows, rows + 2 * edge, 0)
    row_ids, col_ids = ids[None, :], ids[:, None]
    inputs = (query_rows, key_rows, value_rows, out_grad)
    unit = 2 * DH * edge * edge * 6

    packed = pack(inputs, WHOLE_IN)
    arrived = []
    for whole, parts in zip(WHOLE_IN, packed):
        if whole:
            arrived.append([all_to_all(parts[0])])
        else:
            theirs = lax.ppermute(parts[1], "head", swap)
            joined = call(join_kernel, [shape(2, 4, half, DH)] * GROUP, parts[0], theirs)
            arrived.append([hop(block, s) for s, block in enumerate(joined)])

    results = []
    previous = None
    for j in range(chunks):
        whole_in, whole_out = WHOLE_IN[j], WHOLE_OUT[j]
        slots = arrived[j]
        if previous is not None:
            slots, _ = lax.optimization_barrier((slots, previous))
        ext, to_even, to_odd = call(
            functools.partial(gather_kernel, whole_in),
            [shape(4, rows, DH), shape(4, edge, DH), shape(4, edge, DH)],
            *slots,
        )
        even = lax.ppermute(to_even, "blk", plane_pairs(0))
        odd = lax.ppermute(to_odd, "blk", plane_pairs(1))
        res = call(
            functools.partial(interior_kernel, edge),
            shape(4, rows, DH),
            ext,
            row_ids,
            col_ids,
            flops=unit * 7,
            exps=7 * edge * edge,
        )
        back = call(
            functools.partial(edge_kernel, edge, whole_out),
            [shape(2 * GROUP, 4, half, DH)] if whole_out else [shape(2, 4, half, DH)] * GROUP,
            ext,
            even,
            odd,
            res,
            row_ids,
            col_ids,
            scratch=[pltpu.VMEM((4, rows, DH), jnp.bfloat16)],
            flops=unit * 2,
            exps=2 * edge * edge,
        )
        previous = back
        if whole_out:
            back = [all_to_all(back[0])]
        else:
            back = [hop(block, s) for s, block in enumerate(back)]
            away = call(split_kernel, shape(GROUP, 4, half, DH), *back)
            back.append(lax.ppermute(away, "head", swap))
        results.append(back)
    return tuple(unpack(results, WHOLE_OUT, half, width))


def solution(mesh):
    placed = P(("blk", "head"), None)
    return jax.shard_map(
        body,
        mesh=mesh,
        in_specs=(placed, placed, placed, placed, P()),
        out_specs=(placed,) * 4,
        check_vma=False,
    )
```

```python
import functools
import math

import jax
import jax.numpy as jnp
from jax import lax
from jax.experimental import pallas as pl
from jax.experimental.pallas import tpu as pltpu
from jax.sharding import PartitionSpec as P

DH = 128
DOC_MOST = 256
MASKED = -1e30
GROUP = 4
IN_APART = (False, False)
OUT_APART = (False, False)
SCALE = 1.0 / math.sqrt(DH)
VMEM = 12 * 1024 * 1024
PACK_VMEM = 56 * 1024 * 1024
PACK_STEPS = 2
WHOLE = pl.BlockSpec(memory_space=pltpu.VMEM)


def dot_nt(a, b):
    return lax.dot_general(a, b, (((1,), (1,)), ((), ())), preferred_element_type=jnp.float32)


def dot_tn(a, b):
    return lax.dot_general(a, b, (((0,), (0,)), ((), ())), preferred_element_type=jnp.float32)


def dot_nn(a, b):
    return lax.dot_general(a, b, (((1,), (0,)), ((), ())), preferred_element_type=jnp.float32)


def self_attention(queries, keys, values, grads, same):
    scores = dot_nt(keys, queries) * (SCALE * math.log2(math.e))
    scores = jnp.where(same, scores, jnp.float32(MASKED))
    top = jnp.max(scores, axis=0, keepdims=True)
    weights = jnp.exp2(scores - top)
    probs = weights * (1.0 / jnp.sum(weights, axis=0, keepdims=True))
    low = probs.astype(jnp.bfloat16)
    attended = dot_tn(values, low).astype(jnp.bfloat16).astype(jnp.float32)
    delta = jnp.sum(attended * grads.T.astype(jnp.float32), axis=0, keepdims=True)
    score_grad = (probs * (dot_nt(values, grads) - delta)).astype(jnp.bfloat16)
    query_grad = (dot_tn(keys, score_grad) * SCALE).T
    key_grad = dot_nn(score_grad, queries) * SCALE
    value_grad = dot_nn(low, grads)
    return attended.T, query_grad, key_grad, value_grad


def tile_ids(table_ref, first):
    lanes = []
    for row in (first, first + 1):
        inside = (row >= 0) & (row < table_ref.shape[0])
        held = jnp.clip(row, 0, table_ref.shape[0] - 1)
        lanes.append(jnp.where(inside, table_ref[pl.ds(held, 1), :], -1))
    down = [jnp.broadcast_to(lane, (lane.shape[1], lane.shape[1])).T for lane in lanes]
    return jnp.concatenate(down, axis=0), jnp.concatenate(lanes, axis=1)


def across(down):
    return jnp.concatenate([down, down], axis=1)


def boundary_attention(low_rows, high_rows, ids_low, ids_high):
    (low_down, low_lane), (high_down, high_lane) = ids_low, ids_high
    first, last = high_lane[:, 0:1], low_lane[:, -1:]
    from_low, from_high = low_down == first, high_down == last
    member_down = (from_low | from_high).astype(jnp.int32)
    member_lane = ((low_lane == first) | (high_lane == last)).astype(jnp.int32)
    chosen = [
        jnp.where(from_low, a.astype(jnp.float32), b.astype(jnp.float32)).astype(jnp.bfloat16)
        for a, b in zip(low_rows, high_rows)
    ]
    return self_attention(*chosen, across(member_down) == member_lane), from_low, from_high


def interior_kernel(edge, ext_ref, table_ref, res_ref):
    tiles = ext_ref.shape[1] // edge
    plane = lax.axis_index("blk") // GROUP
    ids = [tile_ids(table_ref, (plane * tiles + t) * 2) for t in range(tiles)]

    def rows_of(t):
        return [ext_ref[m, t * edge : (t + 1) * edge] for m in range(4)]

    def put(t, chosen, results):
        at = slice(t * edge, (t + 1) * edge)
        for m, result in enumerate(results):
            if chosen is not None:
                result = jnp.where(chosen, result, res_ref[m, at].astype(jnp.float32))
            res_ref[m, at] = result.astype(jnp.bfloat16)

    for t in range(tiles):
        down, lane = ids[t]
        put(t, None, self_attention(*rows_of(t), across(down) == lane))
        if t > 0:
            results, from_low, from_high = boundary_attention(
                rows_of(t - 1), rows_of(t), ids[t - 1], ids[t]
            )
            put(t - 1, from_low, results)
            put(t, from_high, results)


def edge_kernel(edge, apart, ext_ref, even_ref, odd_ref, res_ref, table_ref, *refs):
    outs, result_ref = refs[:-1], refs[-1]
    rows = ext_ref.shape[1]
    position, core = lax.axis_index("blk"), lax.axis_index("head")
    place, parity = position % GROUP, (position // GROUP) % 2
    result_ref[...] = res_ref[...]

    tiles = rows // edge
    base = (position // GROUP) * tiles

    for side in range(2):
        from_even = parity == (1 - side)
        halo = [jnp.where(from_even, even_ref[m], odd_ref[m]) for m in range(4)]
        own = slice(0, edge) if side == 0 else slice(rows - edge, rows)
        mine = [ext_ref[m, own] for m in range(4)]
        if side == 0:
            results, _, chosen = boundary_attention(
                halo, mine, tile_ids(table_ref, (base - 1) * 2), tile_ids(table_ref, base * 2)
            )
        else:
            results, chosen, _ = boundary_attention(
                mine,
                halo,
                tile_ids(table_ref, (base + tiles - 1) * 2),
                tile_ids(table_ref, (base + tiles) * 2),
            )
        for m, result in enumerate(results):
            result = jnp.where(chosen, result, result_ref[m, own].astype(jnp.float32))
            result_ref[m, own] = result.astype(jnp.bfloat16)
    half = edge // 2
    for s in range(GROUP):
        for piece in range(2):
            first = pl.multiple_of(((place ^ s) * 2 + (core ^ piece)) * half, half)
            block = result_ref[:, pl.ds(first, half), :]
            if apart:
                outs[2 * s + piece][...] = block
            else:
                outs[s][piece] = block


def shape(*dims, dtype=jnp.bfloat16):
    return jax.ShapeDtypeStruct(dims, dtype)


def call(kernel, out_shape, *args, scratch=(), flops=0, exps=0):
    return pl.pallas_call(
        kernel,
        out_shape=out_shape,
        in_specs=[WHOLE] * len(args),
        out_specs=jax.tree.map(lambda _: WHOLE, out_shape),
        scratch_shapes=scratch,
        compiler_params=pltpu.CompilerParams(vmem_limit_bytes=VMEM),
        cost_estimate=pl.CostEstimate(flops=1, bytes_accessed=1, transcendentals=0),
    )(*args)


def pack_kernel(j, chunks, apart, *refs):
    ins, outs = refs[:4], refs[4:]
    block, width = ins[0].shape
    core, place = lax.axis_index("head"), lax.axis_index("blk") % GROUP
    at = pl.ds(pl.multiple_of(pl.program_id(0) * block, block), block)
    for s in range(GROUP):
        for which in range(2):
            base = (core ^ which) * (width // 2) + ((place ^ s) * chunks + j) * DH
            first = pl.multiple_of(base, DH)
            for m, ref in enumerate(ins):
                part = ref[:, pl.ds(first, DH)]
                if apart:
                    outs[2 * s + which][m, at] = part
                else:
                    outs[which][s, m, at] = part


def pack(arrays, j, chunks, apart):
    rows, width = arrays[0].shape
    block = rows // PACK_STEPS
    outs = [shape(4, rows, DH)] * (2 * GROUP) if apart else [shape(GROUP, 4, rows, DH)] * 2
    return pl.pallas_call(
        functools.partial(pack_kernel, j, chunks, apart),
        grid=(PACK_STEPS,),
        out_shape=outs,
        in_specs=[pl.BlockSpec((block, width), lambda i: (i, 0))] * 4,
        out_specs=[WHOLE] * len(outs),
        compiler_params=pltpu.CompilerParams(vmem_limit_bytes=PACK_VMEM),
    )(*arrays)


def join_kernel(mine_ref, received_ref, *outs):
    for s, out in enumerate(outs):
        out[0] = mine_ref[s]
        out[1] = received_ref[s]


def gather_kernel(apart, *refs):
    slots, (ext, to_even, to_odd) = refs[:-3], refs[-3:]
    edge = to_even.shape[1]
    half = edge // 2
    position, core = lax.axis_index("blk"), lax.axis_index("head")
    place, parity = position % GROUP, (position // GROUP) % 2
    for s in range(GROUP):
        for piece in range(2):
            first = pl.multiple_of(((place ^ s) * 2 + (core ^ piece)) * half, half)
            ext[:, pl.ds(first, half), :] = slots[2 * s + piece][...] if apart else slots[s][piece]
    rows = ext.shape[1]
    first = pl.multiple_of((rows - edge) * (1 - parity), edge)
    to_even[...] = ext[:, pl.ds(first, edge), :]
    first = pl.multiple_of((rows - edge) * parity, edge)
    to_odd[...] = ext[:, pl.ds(first, edge), :]


def split_kernel(*refs):
    slots, out = refs[:-1], refs[-1]
    for s, slot in enumerate(slots):
        out[s] = slot[1]


def unpack_kernel(aparts, *refs):
    ins, outs, held, sems = list(refs[:-6]), refs[-6:-2], refs[-2], refs[-1]
    width = outs[0].shape[1]
    chunks = len(aparts)
    core, place = lax.axis_index("head"), lax.axis_index("blk") % GROUP
    blocks = []
    for j, apart in enumerate(aparts):
        slots, ins = (ins[: 2 * GROUP], ins[2 * GROUP :]) if apart else (ins[: GROUP + 1], ins[GROUP + 1 :])
        for s in range(GROUP):
            for which in range(2):
                base = (core ^ which) * (width // 2) + ((place ^ s) * chunks + j) * DH
                if apart:
                    block = slots[2 * s + which]
                else:
                    block = slots[GROUP].at[s] if which else slots[s].at[0]
                blocks.append((pl.multiple_of(base, DH), block))
    copies = [pltpu.make_async_copy(held.at[m], out, sems.at[m]) for m, out in enumerate(outs)]
    for m, copy in enumerate(copies):
        for first, block in blocks:
            held[m, :, pl.ds(first, DH)] = block[m]
        copy.start()
    for copy in copies:
        copy.wait()


def unpack(chunks, aparts, rows, width):
    blocks = [block for chunk in chunks for block in chunk]
    return pl.pallas_call(
        functools.partial(unpack_kernel, aparts),
        out_shape=[shape(rows, width)] * 4,
        in_specs=[WHOLE] * len(blocks),
        out_specs=[pl.BlockSpec(memory_space=pl.ANY)] * 4,
        scratch_shapes=[
            pltpu.VMEM((4, rows, width), jnp.bfloat16),
            pltpu.SemaphoreType.DMA((4,)),
        ],
        compiler_params=pltpu.CompilerParams(vmem_limit_bytes=VMEM),
    )(*blocks)


def body(query_rows, key_rows, value_rows, out_grad, doc_ids):
    positions = lax.axis_size("blk")
    half, width = query_rows.shape
    heads = width // DH
    chunks = heads // (2 * GROUP)
    edge = 2 * half
    rows = GROUP * edge
    assert edge >= DOC_MOST and positions % GROUP == 0 and chunks == len(IN_APART)
    swap = [(0, 1), (1, 0)]
    planes = positions // GROUP

    def plane_pairs(first):
        route = []
        for low in range(first, planes - 1, 2):
            for i in range(GROUP):
                here, there = low * GROUP + i, (low + 1) * GROUP + i
                route += [(here, there), (there, here)]
        return route

    def hop(block, s, cross=0):
        if s == 0:
            return lax.ppermute(block, "head", swap) if cross else block
        if not cross:
            return lax.ppermute(block, "blk", [(i, i ^ s) for i in range(positions)])
        route = [(2 * i + k, 2 * (i ^ s) + 1 - k) for i in range(positions) for k in range(2)]
        return lax.ppermute(block, ("blk", "head"), route)

    table = doc_ids.reshape(-1, half)
    inputs = (query_rows, key_rows, value_rows, out_grad)
    unit = 2 * DH * edge * edge * 6

    arrived = []
    for j, apart in enumerate(IN_APART):
        packed = pack(inputs, j, chunks, apart)
        if apart:
            arrived.append([hop(block, *divmod(i, 2)) for i, block in enumerate(packed)])
        else:
            theirs = lax.ppermute(packed[1], "head", swap)
            joined = call(join_kernel, [shape(2, 4, half, DH)] * GROUP, packed[0], theirs)
            arrived.append([hop(block, s) for s, block in enumerate(joined)])

    def gather(j, *after):
        slots = arrived[j]
        if after:
            slots, _ = lax.optimization_barrier((slots, after))
        return call(
            functools.partial(gather_kernel, IN_APART[j]),
            [shape(4, rows, DH), shape(4, edge, DH), shape(4, edge, DH)],
            *slots,
        )

    def halo(to_even, to_odd):
        even = lax.ppermute(to_even, "blk", plane_pairs(0))
        return even, lax.ppermute(to_odd, "blk", plane_pairs(1))

    def interior(ext):
        return call(
            functools.partial(interior_kernel, edge), shape(4, rows, DH), ext, table
        )

    def finish(j, ext, even, odd, res):
        apart = OUT_APART[j]
        return call(
            functools.partial(edge_kernel, edge, apart),
            [shape(4, half, DH)] * (2 * GROUP) if apart else [shape(2, 4, half, DH)] * GROUP,
            ext,
            even,
            odd,
            res,
            table,
            scratch=[pltpu.VMEM((4, rows, DH), jnp.bfloat16)],
        )

    def give_back(j, back):
        if OUT_APART[j]:
            return [hop(block, *divmod(i, 2)) for i, block in enumerate(back)]
        back = [hop(block, s) for s, block in enumerate(back)]
        away = call(split_kernel, shape(GROUP, 4, half, DH), *back)
        return back + [lax.ppermute(away, "head", swap)]

    ext_a, *edges_a = gather(0)
    halo_a = halo(*edges_a)
    res_a = interior(ext_a)
    ext_b, *edges_b = gather(1, res_a)
    res_a, ext_b = lax.optimization_barrier((res_a, ext_b))
    back_a = finish(0, ext_a, *halo_a, res_a)
    ext_b, edges_b, back_a = lax.optimization_barrier((ext_b, edges_b, back_a))
    halo_b = halo(*edges_b)
    res_b = interior(ext_b)
    back_b = finish(1, ext_b, *halo_b, res_b)
    results = [give_back(0, back_a), give_back(1, back_b)]
    return tuple(unpack(results, OUT_APART, half, width))


def solution(mesh):
    placed = P(("blk", "head"), None)
    return jax.shard_map(
        body,
        mesh=mesh,
        in_specs=(placed, placed, placed, placed, P()),
        out_specs=(placed,) * 4,
        check_vma=False,
    )
```

```python
import functools
import math

import jax
import jax.numpy as jnp
from jax import lax
from jax.experimental import pallas as pl
from jax.experimental.pallas import tpu as pltpu
from jax.sharding import PartitionSpec as P

DH = 128
DOC_MOST = 256
MASKED = -1e30
GROUP = 4
ORDER_IN = (0, 3, 2, 1)
ORDER_OUT = (0, 2, 1, 3)
SCALE = 1.0 / math.sqrt(DH)
VMEM = 12 * 1024 * 1024
PACK_VMEM = 56 * 1024 * 1024
PACK_STEPS = 2
WHOLE = pl.BlockSpec(memory_space=pltpu.VMEM)


def dot_nt(a, b):
    return lax.dot_general(a, b, (((1,), (1,)), ((), ())), preferred_element_type=jnp.float32)


def dot_tn(a, b):
    return lax.dot_general(a, b, (((0,), (0,)), ((), ())), preferred_element_type=jnp.float32)


def dot_nn(a, b):
    return lax.dot_general(a, b, (((1,), (0,)), ((), ())), preferred_element_type=jnp.float32)


def self_attention(queries, keys, values, grads, same):
    scores = dot_nt(keys, queries) * (SCALE * math.log2(math.e))
    scores = jnp.where(same, scores, jnp.float32(MASKED))
    top = jnp.max(scores, axis=0, keepdims=True)
    weights = jnp.exp2(scores - top)
    probs = weights * (1.0 / jnp.sum(weights, axis=0, keepdims=True))
    low = probs.astype(jnp.bfloat16)
    weighted = probs * dot_nt(values, grads)
    delta = jnp.sum(weighted, axis=0, keepdims=True)
    score_grad = (weighted - probs * delta).astype(jnp.bfloat16)
    attended = dot_tn(values, low).T
    query_grad = (dot_tn(keys, score_grad) * SCALE).T
    key_grad = dot_nn(score_grad, queries) * SCALE
    value_grad = dot_nn(low, grads)
    return attended, query_grad, key_grad, value_grad


def tile_ids(table_ref, first):
    lanes = []
    for row in (first, first + 1):
        inside = (row >= 0) & (row < table_ref.shape[0])
        held = jnp.clip(row, 0, table_ref.shape[0] - 1)
        lanes.append(jnp.where(inside, table_ref[pl.ds(held, 1), :], -1))
    down = [jnp.broadcast_to(lane, (lane.shape[1], lane.shape[1])).T for lane in lanes]
    return jnp.concatenate(down, axis=0), jnp.concatenate(lanes, axis=1)


def across(down):
    return jnp.concatenate([down, down], axis=1)


def boundary_attention(low_rows, high_rows, ids_low, ids_high):
    (low_down, low_lane), (high_down, high_lane) = ids_low, ids_high
    first, last = high_lane[:, 0:1], low_lane[:, -1:]
    from_low, from_high = low_down == first, high_down == last
    member_down = (from_low | from_high).astype(jnp.int32)
    member_lane = ((low_lane == first) | (high_lane == last)).astype(jnp.int32)
    chosen = [
        jnp.where(from_low, a.astype(jnp.float32), b.astype(jnp.float32)).astype(jnp.bfloat16)
        for a, b in zip(low_rows, high_rows)
    ]
    return self_attention(*chosen, across(member_down) == member_lane), from_low, from_high


def interior_kernel(edge, ext_ref, table_ref, res_ref):
    tiles = ext_ref.shape[1] // edge
    plane = lax.axis_index("blk") // GROUP
    ids = [tile_ids(table_ref, (plane * tiles + t) * 2) for t in range(tiles)]

    def rows_of(t):
        return [ext_ref[m, t * edge : (t + 1) * edge] for m in range(4)]

    def put(t, chosen, results):
        at = slice(t * edge, (t + 1) * edge)
        for m, result in enumerate(results):
            if chosen is not None:
                result = jnp.where(chosen, result, res_ref[m, at].astype(jnp.float32))
            res_ref[m, at] = result.astype(jnp.bfloat16)

    for t in range(tiles):
        down, lane = ids[t]
        put(t, None, self_attention(*rows_of(t), across(down) == lane))
        if t > 0:
            results, from_low, from_high = boundary_attention(
                rows_of(t - 1), rows_of(t), ids[t - 1], ids[t]
            )
            put(t - 1, from_low, results)
            put(t, from_high, results)


def edge_kernel(edge, ext_ref, even_ref, odd_ref, res_ref, table_ref, *refs):
    outs, result_ref = refs[:-1], refs[-1]
    rows = ext_ref.shape[1]
    position, core = lax.axis_index("blk"), lax.axis_index("head")
    place, parity = position % GROUP, (position // GROUP) % 2
    result_ref[...] = res_ref[...]

    tiles = rows // edge
    base = (position // GROUP) * tiles

    for side in range(2):
        from_even = parity == (1 - side)
        halo = [jnp.where(from_even, even_ref[m], odd_ref[m]) for m in range(4)]
        own = slice(0, edge) if side == 0 else slice(rows - edge, rows)
        mine = [ext_ref[m, own] for m in range(4)]
        if side == 0:
            results, _, chosen = boundary_attention(
                halo, mine, tile_ids(table_ref, (base - 1) * 2), tile_ids(table_ref, base * 2)
            )
        else:
            results, chosen, _ = boundary_attention(
                mine,
                halo,
                tile_ids(table_ref, (base + tiles - 1) * 2),
                tile_ids(table_ref, (base + tiles) * 2),
            )
        for m, result in enumerate(results):
            result = jnp.where(chosen, result, result_ref[m, own].astype(jnp.float32))
            result_ref[m, own] = result.astype(jnp.bfloat16)
    half = edge // 2
    for s in range(GROUP):
        for piece in range(2):
            first = pl.multiple_of(((place ^ s) * 2 + (core ^ piece)) * half, half)
            outs[s][piece] = result_ref[:, pl.ds(first, half), :]


def shape(*dims, dtype=jnp.bfloat16):
    return jax.ShapeDtypeStruct(dims, dtype)


def call(kernel, out_shape, *args, scratch=(), flops=0, exps=0):
    return pl.pallas_call(
        kernel,
        out_shape=out_shape,
        in_specs=[WHOLE] * len(args),
        out_specs=jax.tree.map(lambda _: WHOLE, out_shape),
        scratch_shapes=scratch,
        compiler_params=pltpu.CompilerParams(vmem_limit_bytes=VMEM),
        cost_estimate=pl.CostEstimate(flops=1, bytes_accessed=1, transcendentals=0),
    )(*args)


def pack_kernel(j, chunks, *refs):
    ins, outs = refs[:4], refs[4:]
    block, width = ins[0].shape
    core, place = lax.axis_index("head"), lax.axis_index("blk") % GROUP
    at = pl.ds(pl.multiple_of(pl.program_id(0) * block, block), block)
    for s in range(GROUP):
        for which in range(2):
            base = (core ^ which) * (width // 2) + ((place ^ s) * chunks + j) * DH
            first = pl.multiple_of(base, DH)
            for m, ref in enumerate(ins):
                outs[which][s, m, at] = ref[:, pl.ds(first, DH)]


def pack(arrays, j, chunks):
    rows, width = arrays[0].shape
    block = rows // PACK_STEPS
    outs = [shape(GROUP, 4, rows, DH)] * 2
    return pl.pallas_call(
        functools.partial(pack_kernel, j, chunks),
        grid=(PACK_STEPS,),
        out_shape=outs,
        in_specs=[pl.BlockSpec((block, width), lambda i: (i, 0))] * 4,
        out_specs=[WHOLE] * len(outs),
        compiler_params=pltpu.CompilerParams(vmem_limit_bytes=PACK_VMEM),
    )(*arrays)


def join_kernel(mine_ref, received_ref, *outs):
    for s, out in enumerate(outs):
        out[0] = mine_ref[s]
        out[1] = received_ref[s]


def gather_kernel(*refs):
    slots, (ext, to_even, to_odd) = refs[:-3], refs[-3:]
    edge = to_even.shape[1]
    half = edge // 2
    position, core = lax.axis_index("blk"), lax.axis_index("head")
    place, parity = position % GROUP, (position // GROUP) % 2
    for s, slot in zip(ORDER_IN, slots):
        for piece in range(2):
            first = pl.multiple_of(((place ^ s) * 2 + (core ^ piece)) * half, half)
            ext[:, pl.ds(first, half), :] = slot[piece]
    rows = ext.shape[1]
    first = pl.multiple_of((rows - edge) * (1 - parity), edge)
    to_even[...] = ext[:, pl.ds(first, edge), :]
    first = pl.multiple_of((rows - edge) * parity, edge)
    to_odd[...] = ext[:, pl.ds(first, edge), :]


def split_kernel(*refs):
    slots, out = refs[:-1], refs[-1]
    for s, slot in zip(ORDER_OUT, slots):
        out[s] = slot[1]


def unpack_kernel(chunks, *refs):
    ins, outs, held, sems = refs[:-6], refs[-6:-2], refs[-2], refs[-1]
    width = outs[0].shape[1]
    core, place = lax.axis_index("head"), lax.axis_index("blk") % GROUP
    blocks = []
    for j in range(chunks):
        *slots, received = ins[j * (GROUP + 1) : (j + 1) * (GROUP + 1)]
        for s, slot in zip(ORDER_OUT, slots):
            for which, block in enumerate((slot.at[0], received.at[s])):
                base = (core ^ which) * (width // 2) + ((place ^ s) * chunks + j) * DH
                blocks.append((pl.multiple_of(base, DH), block))
    copies = [pltpu.make_async_copy(held.at[m], out, sems.at[m]) for m, out in enumerate(outs)]
    for m, copy in enumerate(copies):
        for first, block in blocks:
            held[m, :, pl.ds(first, DH)] = block[m]
        copy.start()
    for copy in copies:
        copy.wait()


def unpack(chunks, rows, width):
    blocks = [block for chunk in chunks for block in chunk]
    return pl.pallas_call(
        functools.partial(unpack_kernel, len(chunks)),
        out_shape=[shape(rows, width)] * 4,
        in_specs=[WHOLE] * len(blocks),
        out_specs=[pl.BlockSpec(memory_space=pl.ANY)] * 4,
        scratch_shapes=[
            pltpu.VMEM((4, rows, width), jnp.bfloat16),
            pltpu.SemaphoreType.DMA((4,)),
        ],
        compiler_params=pltpu.CompilerParams(vmem_limit_bytes=VMEM),
    )(*blocks)


def body(query_rows, key_rows, value_rows, out_grad, doc_ids):
    positions = lax.axis_size("blk")
    half, width = query_rows.shape
    heads = width // DH
    chunks = heads // (2 * GROUP)
    edge = 2 * half
    rows = GROUP * edge
    assert edge >= DOC_MOST and positions % GROUP == 0 and chunks == 2
    swap = [(0, 1), (1, 0)]
    planes = positions // GROUP

    def plane_pairs(first):
        route = []
        for low in range(first, planes - 1, 2):
            for i in range(GROUP):
                here, there = low * GROUP + i, (low + 1) * GROUP + i
                route += [(here, there), (there, here)]
        return route

    def hop(block, s):
        return lax.ppermute(block, "blk", [(i, i ^ s) for i in range(positions)]) if s else block

    table = doc_ids.reshape(-1, half)
    inputs = (query_rows, key_rows, value_rows, out_grad)
    unit = 2 * DH * edge * edge * 6

    arrived = []
    for j in range(chunks):
        mine, other = pack(inputs, j, chunks)
        theirs = lax.ppermute(other, "head", swap)
        joined = call(join_kernel, [shape(2, 4, half, DH)] * GROUP, mine, theirs)
        arrived.append([hop(joined[s], s) for s in ORDER_IN])

    def gather(j, *after):
        slots = arrived[j]
        if after:
            slots, _ = lax.optimization_barrier((slots, after))
        return call(
            gather_kernel,
            [shape(4, rows, DH), shape(4, edge, DH), shape(4, edge, DH)],
            *slots,
        )

    def halo(to_even, to_odd):
        even = lax.ppermute(to_even, "blk", plane_pairs(0))
        return even, lax.ppermute(to_odd, "blk", plane_pairs(1))

    def interior(ext):
        return call(
            functools.partial(interior_kernel, edge), shape(4, rows, DH), ext, table
        )

    def finish(ext, even, odd, res):
        return call(
            functools.partial(edge_kernel, edge),
            [shape(2, 4, half, DH)] * GROUP,
            ext,
            even,
            odd,
            res,
            table,
            scratch=[pltpu.VMEM((4, rows, DH), jnp.bfloat16)],
        )

    def give_back(back):
        return [hop(back[s], s) for s in ORDER_OUT]

    def swap_back(back):
        away = call(split_kernel, shape(GROUP, 4, half, DH), *back)
        return back + [lax.ppermute(away, "head", swap)]

    ext_a, *edges_a = gather(0)
    halo_a = halo(*edges_a)
    res_a = interior(ext_a)
    ext_b, *edges_b = gather(1, res_a)
    res_a, ext_b = lax.optimization_barrier((res_a, ext_b))
    back_a = finish(ext_a, *halo_a, res_a)
    ext_b, edges_b, back_a = lax.optimization_barrier((ext_b, edges_b, back_a))
    halo_b = halo(*edges_b)
    res_b = interior(ext_b)
    out_a = give_back(back_a)
    res_b, tied = lax.optimization_barrier((res_b, [out_a[i] for i in (1, 2)]))
    for i, block in zip((1, 2), tied):
        out_a[i] = block
    back_b = finish(ext_b, *halo_b, res_b)
    out_b = give_back(back_b)
    results = [swap_back(out_a), swap_back(out_b)]
    return tuple(unpack(results, half, width))


def solution(mesh):
    placed = P(("blk", "head"), None)
    return jax.shard_map(
        body,
        mesh=mesh,
        in_specs=(placed, placed, placed, placed, P()),
        out_specs=(placed,) * 4,
        check_vma=False,
    )
```

```python
import functools
import math

import jax
import jax.numpy as jnp
from jax import lax
from jax.experimental import pallas as pl
from jax.experimental.pallas import tpu as pltpu
from jax.sharding import PartitionSpec as P

DH = 128
DOC_MOST = 256
MASKED = -1e30
GROUP = 4
ORDER_IN = (0, 3, 2, 1)
ORDER_OUT = (0, 2, 1, 3)
SCALE = 1.0 / math.sqrt(DH)
VMEM = 12 * 1024 * 1024
PACK_VMEM = 56 * 1024 * 1024
PACK_STEPS = 2
WHOLE = pl.BlockSpec(memory_space=pltpu.VMEM)


def dot_nt(a, b):
    return lax.dot_general(a, b, (((1,), (1,)), ((), ())), preferred_element_type=jnp.float32)


def dot_tn(a, b):
    return lax.dot_general(a, b, (((0,), (0,)), ((), ())), preferred_element_type=jnp.float32)


def dot_nn(a, b):
    return lax.dot_general(a, b, (((1,), (0,)), ((), ())), preferred_element_type=jnp.float32)


def self_attention(queries, keys, values, grads, same):
    scores = dot_nt(keys, queries) * (SCALE * math.log2(math.e))
    scores = jnp.where(same, scores, jnp.float32(MASKED))
    top = jnp.max(scores, axis=0, keepdims=True)
    weights = jnp.exp2(scores - top)
    probs = weights * (1.0 / jnp.sum(weights, axis=0, keepdims=True))
    low = probs.astype(jnp.bfloat16)
    weighted = probs * dot_nt(values, grads)
    delta = jnp.sum(weighted, axis=0, keepdims=True)
    score_grad = (weighted - probs * delta).astype(jnp.bfloat16)
    attended = dot_tn(values, low).T
    query_grad = (dot_tn(keys, score_grad) * SCALE).T
    key_grad = dot_nn(score_grad, queries) * SCALE
    value_grad = dot_nn(low, grads)
    return attended, query_grad, key_grad, value_grad


def tile_ids(table_ref, first):
    lanes = []
    for row in (first, first + 1):
        inside = (row >= 0) & (row < table_ref.shape[0])
        held = jnp.clip(row, 0, table_ref.shape[0] - 1)
        lanes.append(jnp.where(inside, table_ref[pl.ds(held, 1), :], -1))
    down = [jnp.broadcast_to(lane, (lane.shape[1], lane.shape[1])).T for lane in lanes]
    return jnp.concatenate(down, axis=0), jnp.concatenate(lanes, axis=1)


def across(down):
    return jnp.concatenate([down, down], axis=1)


def boundary_attention(low_rows, high_rows, ids_low, ids_high):
    (low_down, low_lane), (high_down, high_lane) = ids_low, ids_high
    first, last = high_lane[:, 0:1], low_lane[:, -1:]
    from_low, from_high = low_down == first, high_down == last
    member_down = (from_low | from_high).astype(jnp.int32)
    member_lane = ((low_lane == first) | (high_lane == last)).astype(jnp.int32)
    chosen = [
        jnp.where(from_low, a.astype(jnp.float32), b.astype(jnp.float32)).astype(jnp.bfloat16)
        for a, b in zip(low_rows, high_rows)
    ]
    return self_attention(*chosen, across(member_down) == member_lane), from_low, from_high


def interior_kernel(edge, ext_ref, table_ref, res_ref):
    tiles = ext_ref.shape[1] // edge
    plane = lax.axis_index("blk") // GROUP
    ids = [tile_ids(table_ref, (plane * tiles + t) * 2) for t in range(tiles)]

    def rows_of(t):
        return [ext_ref[m, t * edge : (t + 1) * edge] for m in range(4)]

    def put(t, chosen, results):
        at = slice(t * edge, (t + 1) * edge)
        for m, result in enumerate(results):
            if chosen is not None:
                result = jnp.where(chosen, result, res_ref[m, at].astype(jnp.float32))
            res_ref[m, at] = result.astype(jnp.bfloat16)

    for t in range(tiles):
        down, lane = ids[t]
        put(t, None, self_attention(*rows_of(t), across(down) == lane))
        if t > 0:
            results, from_low, from_high = boundary_attention(
                rows_of(t - 1), rows_of(t), ids[t - 1], ids[t]
            )
            put(t - 1, from_low, results)
            put(t, from_high, results)


def edge_kernel(edge, ext_ref, even_ref, odd_ref, res_ref, table_ref, *refs):
    outs, result_ref = refs[:-1], refs[-1]
    rows = ext_ref.shape[1]
    position, core = lax.axis_index("blk"), lax.axis_index("head")
    place, parity = position % GROUP, (position // GROUP) % 2
    result_ref[...] = res_ref[...]

    tiles = rows // edge
    base = (position // GROUP) * tiles

    for side in range(2):
        from_even = parity == (1 - side)
        halo = [jnp.where(from_even, even_ref[m], odd_ref[m]) for m in range(4)]
        own = slice(0, edge) if side == 0 else slice(rows - edge, rows)
        mine = [ext_ref[m, own] for m in range(4)]
        if side == 0:
            results, _, chosen = boundary_attention(
                halo, mine, tile_ids(table_ref, (base - 1) * 2), tile_ids(table_ref, base * 2)
            )
        else:
            results, chosen, _ = boundary_attention(
                mine,
                halo,
                tile_ids(table_ref, (base + tiles - 1) * 2),
                tile_ids(table_ref, (base + tiles) * 2),
            )
        for m, result in enumerate(results):
            result = jnp.where(chosen, result, result_ref[m, own].astype(jnp.float32))
            result_ref[m, own] = result.astype(jnp.bfloat16)
    half = edge // 2
    for s in range(GROUP):
        for piece in range(2):
            first = pl.multiple_of(((place ^ s) * 2 + (core ^ piece)) * half, half)
            outs[s][piece] = result_ref[:, pl.ds(first, half), :]


def shape(*dims, dtype=jnp.bfloat16):
    return jax.ShapeDtypeStruct(dims, dtype)


def call(kernel, out_shape, *args, scratch=(), flops=0, exps=0):
    return pl.pallas_call(
        kernel,
        out_shape=out_shape,
        in_specs=[WHOLE] * len(args),
        out_specs=jax.tree.map(lambda _: WHOLE, out_shape),
        scratch_shapes=scratch,
        compiler_params=pltpu.CompilerParams(vmem_limit_bytes=VMEM),
        cost_estimate=pl.CostEstimate(flops=1, bytes_accessed=1, transcendentals=0),
    )(*args)


def pack_kernel(j, chunks, *refs):
    ins, outs = refs[:4], refs[4:]
    block, width = ins[0].shape
    core, place = lax.axis_index("head"), lax.axis_index("blk") % GROUP
    at = pl.ds(pl.multiple_of(pl.program_id(0) * block, block), block)
    for s in range(GROUP):
        for which in range(2):
            base = (core ^ which) * (width // 2) + ((place ^ s) * chunks + j) * DH
            first = pl.multiple_of(base, DH)
            for m, ref in enumerate(ins):
                outs[which][s, m, at] = ref[:, pl.ds(first, DH)]


def pack(arrays, j, chunks):
    rows, width = arrays[0].shape
    block = rows // PACK_STEPS
    outs = [shape(GROUP, 4, rows, DH)] * 2
    return pl.pallas_call(
        functools.partial(pack_kernel, j, chunks),
        grid=(PACK_STEPS,),
        out_shape=outs,
        in_specs=[pl.BlockSpec((block, width), lambda i: (i, 0))] * 4,
        out_specs=[WHOLE] * len(outs),
        compiler_params=pltpu.CompilerParams(vmem_limit_bytes=PACK_VMEM),
    )(*arrays)


def join_kernel(mine_ref, received_ref, *outs):
    for s, out in enumerate(outs):
        out[0] = mine_ref[s]
        out[1] = received_ref[s]


def gather_kernel(*refs):
    slots, (ext, to_even, to_odd) = refs[:-3], refs[-3:]
    edge = to_even.shape[1]
    half = edge // 2
    position, core = lax.axis_index("blk"), lax.axis_index("head")
    place, parity = position % GROUP, (position // GROUP) % 2
    for s, slot in zip(ORDER_IN, slots):
        for piece in range(2):
            first = pl.multiple_of(((place ^ s) * 2 + (core ^ piece)) * half, half)
            ext[:, pl.ds(first, half), :] = slot[piece]
    rows = ext.shape[1]
    first = pl.multiple_of((rows - edge) * (1 - parity), edge)
    to_even[...] = ext[:, pl.ds(first, edge), :]
    first = pl.multiple_of((rows - edge) * parity, edge)
    to_odd[...] = ext[:, pl.ds(first, edge), :]


def split_kernel(*refs):
    slots, out = refs[:-1], refs[-1]
    for s, slot in zip(ORDER_OUT, slots):
        out[s] = slot[1]


def unpack_kernel(chunks, *refs):
    ins, outs, held, sems = refs[:-6], refs[-6:-2], refs[-2], refs[-1]
    width = outs[0].shape[1]
    core, place = lax.axis_index("head"), lax.axis_index("blk") % GROUP
    blocks = []
    for j in range(chunks):
        *slots, received = ins[j * (GROUP + 1) : (j + 1) * (GROUP + 1)]
        for s, slot in zip(ORDER_OUT, slots):
            for which, block in enumerate((slot.at[0], received.at[s])):
                base = (core ^ which) * (width // 2) + ((place ^ s) * chunks + j) * DH
                blocks.append((pl.multiple_of(base, DH), block))
    copies = [pltpu.make_async_copy(held.at[m], out, sems.at[m]) for m, out in enumerate(outs)]
    for m, copy in enumerate(copies):
        for first, block in blocks:
            held[m, :, pl.ds(first, DH)] = block[m]
        copy.start()
    for copy in copies:
        copy.wait()


def unpack(chunks, rows, width):
    blocks = [block for chunk in chunks for block in chunk]
    return pl.pallas_call(
        functools.partial(unpack_kernel, len(chunks)),
        out_shape=[shape(rows, width)] * 4,
        in_specs=[WHOLE] * len(blocks),
        out_specs=[pl.BlockSpec(memory_space=pl.ANY)] * 4,
        scratch_shapes=[
            pltpu.VMEM((4, rows, width), jnp.bfloat16),
            pltpu.SemaphoreType.DMA((4,)),
        ],
        compiler_params=pltpu.CompilerParams(vmem_limit_bytes=VMEM),
    )(*blocks)


def body(query_rows, key_rows, value_rows, out_grad, doc_ids):
    positions = lax.axis_size("blk")
    half, width = query_rows.shape
    heads = width // DH
    chunks = heads // (2 * GROUP)
    edge = 2 * half
    rows = GROUP * edge
    assert edge >= DOC_MOST and positions % GROUP == 0 and chunks == 2
    swap = [(0, 1), (1, 0)]
    planes = positions // GROUP

    def plane_pairs(first):
        route = []
        for low in range(first, planes - 1, 2):
            for i in range(GROUP):
                here, there = low * GROUP + i, (low + 1) * GROUP + i
                route += [(here, there), (there, here)]
        return route

    def hop(block, s):
        return lax.ppermute(block, "blk", [(i, i ^ s) for i in range(positions)]) if s else block

    table = doc_ids.reshape(-1, half)
    inputs = (query_rows, key_rows, value_rows, out_grad)
    unit = 2 * DH * edge * edge * 6

    arrived = []
    for j in range(chunks):
        mine, other = pack(inputs, j, chunks)
        theirs = lax.ppermute(other, "head", swap)
        joined = call(join_kernel, [shape(2, 4, half, DH)] * GROUP, mine, theirs)
        arrived.append([hop(joined[s], s) for s in ORDER_IN])

    def gather(j, *after):
        slots = arrived[j]
        if after:
            slots, _ = lax.optimization_barrier((slots, after))
        return call(
            gather_kernel,
            [shape(4, rows, DH), shape(4, edge, DH), shape(4, edge, DH)],
            *slots,
        )

    def halo(to_even, to_odd):
        even = lax.ppermute(to_even, "blk", plane_pairs(0))
        return even, lax.ppermute(to_odd, "blk", plane_pairs(1))

    def interior(ext):
        return call(
            functools.partial(interior_kernel, edge), shape(4, rows, DH), ext, table
        )

    def finish(ext, even, odd, res):
        return call(
            functools.partial(edge_kernel, edge),
            [shape(2, 4, half, DH)] * GROUP,
            ext,
            even,
            odd,
            res,
            table,
            scratch=[pltpu.VMEM((4, rows, DH), jnp.bfloat16)],
        )

    def give_back(back):
        return [hop(back[s], s) for s in ORDER_OUT]

    def swap_back(back):
        away = call(split_kernel, shape(GROUP, 4, half, DH), *back)
        return back + [lax.ppermute(away, "head", swap)]

    ext_a, *edges_a = gather(0)
    halo_a = halo(*edges_a)
    res_a = interior(ext_a)
    res_a, arrived[1][1] = lax.optimization_barrier((res_a, arrived[1][1]))
    back_a = finish(ext_a, *halo_a, res_a)
    ext_b, *edges_b = gather(1, back_a)
    halo_b = halo(*edges_b)
    res_b = interior(ext_b)
    out_a = give_back(back_a)
    res_b, tied = lax.optimization_barrier((res_b, [out_a[i] for i in (1, 2)]))
    for i, block in zip((1, 2), tied):
        out_a[i] = block
    back_b = finish(ext_b, *halo_b, res_b)
    out_b = give_back(back_b)
    results = [swap_back(out_a), swap_back(out_b)]
    return tuple(unpack(results, half, width))


def solution(mesh):
    placed = P(("blk", "head"), None)
    return jax.shard_map(
        body,
        mesh=mesh,
        in_specs=(placed, placed, placed, placed, P()),
        out_specs=(placed,) * 4,
        check_vma=False,
    )
```

```python
import functools
import math

import jax
import jax.numpy as jnp
from jax import lax
from jax.experimental import pallas as pl
from jax.experimental.pallas import tpu as pltpu
from jax.sharding import PartitionSpec as P

DH = 128
DOC_MOST = 256
MASKED = -1e30
GROUP = 4
ORDER_IN = (0, 3, 2, 1)
ORDER_OUT = (0, 2, 1, 3)
SCALE = 1.0 / math.sqrt(DH)
VMEM = 12 * 1024 * 1024
PACK_VMEM = 53 * 1024 * 1024
PACK_STEPS = 2
WHOLE = pl.BlockSpec(memory_space=pltpu.VMEM)


def dot_nt(a, b):
    return lax.dot_general(a, b, (((1,), (1,)), ((), ())), preferred_element_type=jnp.float32)


def dot_tn(a, b):
    return lax.dot_general(a, b, (((0,), (0,)), ((), ())), preferred_element_type=jnp.float32)


def dot_nn(a, b):
    return lax.dot_general(a, b, (((1,), (0,)), ((), ())), preferred_element_type=jnp.float32)


def self_attention(queries, keys, values, grads, same):
    scores = dot_nt(keys, queries) * (SCALE * math.log2(math.e))
    scores = jnp.where(same, scores, jnp.float32(MASKED))
    top = jnp.max(scores, axis=0, keepdims=True)
    weights = jnp.exp2(scores - top)
    probs = weights * (1.0 / jnp.sum(weights, axis=0, keepdims=True))
    low = probs.astype(jnp.bfloat16)
    weighted = probs * dot_nt(values, grads)
    delta = jnp.sum(weighted, axis=0, keepdims=True)
    score_grad = (weighted - probs * delta).astype(jnp.bfloat16)
    attended = dot_tn(values, low).T
    query_grad = (dot_tn(keys, score_grad) * SCALE).T
    key_grad = dot_nn(score_grad, queries) * SCALE
    value_grad = dot_nn(low, grads)
    return attended, query_grad, key_grad, value_grad


def tile_ids(table_ref, first):
    lanes = []
    for row in (first, first + 1):
        inside = (row >= 0) & (row < table_ref.shape[0])
        held = jnp.clip(row, 0, table_ref.shape[0] - 1)
        lanes.append(jnp.where(inside, table_ref[pl.ds(held, 1), :], -1))
    down = [jnp.broadcast_to(lane, (lane.shape[1], lane.shape[1])).T for lane in lanes]
    return jnp.concatenate(down, axis=0), jnp.concatenate(lanes, axis=1)


def across(down):
    return jnp.concatenate([down, down], axis=1)


def boundary_attention(low_rows, high_rows, ids_low, ids_high):
    (low_down, low_lane), (high_down, high_lane) = ids_low, ids_high
    first, last = high_lane[:, 0:1], low_lane[:, -1:]
    from_low, from_high = low_down == first, high_down == last
    member_down = (from_low | from_high).astype(jnp.int32)
    member_lane = ((low_lane == first) | (high_lane == last)).astype(jnp.int32)
    chosen = [
        jnp.where(from_low, a.astype(jnp.float32), b.astype(jnp.float32)).astype(jnp.bfloat16)
        for a, b in zip(low_rows, high_rows)
    ]
    return self_attention(*chosen, across(member_down) == member_lane), from_low, from_high


def interior_kernel(edge, ext_ref, table_ref, res_ref):
    tiles = ext_ref.shape[1] // edge
    plane = lax.axis_index("blk") // GROUP
    ids = [tile_ids(table_ref, (plane * tiles + t) * 2) for t in range(tiles)]

    def rows_of(t):
        return [ext_ref[m, t * edge : (t + 1) * edge] for m in range(4)]

    def put(t, chosen, results):
        at = slice(t * edge, (t + 1) * edge)
        for m, result in enumerate(results):
            if chosen is not None:
                result = jnp.where(chosen, result, res_ref[m, at].astype(jnp.float32))
            res_ref[m, at] = result.astype(jnp.bfloat16)

    for t in range(tiles):
        down, lane = ids[t]
        put(t, None, self_attention(*rows_of(t), across(down) == lane))
        if t > 0:
            results, from_low, from_high = boundary_attention(
                rows_of(t - 1), rows_of(t), ids[t - 1], ids[t]
            )
            put(t - 1, from_low, results)
            put(t, from_high, results)


def edge_kernel(edge, ext_ref, even_ref, odd_ref, res_ref, table_ref, *refs):
    outs, result_ref = refs[:-1], refs[-1]
    rows = ext_ref.shape[1]
    position, core = lax.axis_index("blk"), lax.axis_index("head")
    place, parity = position % GROUP, (position // GROUP) % 2
    result_ref[...] = res_ref[...]

    tiles = rows // edge
    base = (position // GROUP) * tiles

    for side in range(2):
        from_even = parity == (1 - side)
        halo = [jnp.where(from_even, even_ref[m], odd_ref[m]) for m in range(4)]
        own = slice(0, edge) if side == 0 else slice(rows - edge, rows)
        mine = [ext_ref[m, own] for m in range(4)]
        if side == 0:
            results, _, chosen = boundary_attention(
                halo, mine, tile_ids(table_ref, (base - 1) * 2), tile_ids(table_ref, base * 2)
            )
        else:
            results, chosen, _ = boundary_attention(
                mine,
                halo,
                tile_ids(table_ref, (base + tiles - 1) * 2),
                tile_ids(table_ref, (base + tiles) * 2),
            )
        for m, result in enumerate(results):
            result = jnp.where(chosen, result, result_ref[m, own].astype(jnp.float32))
            result_ref[m, own] = result.astype(jnp.bfloat16)
    half = edge // 2
    for s in range(GROUP):
        for piece in range(2):
            first = pl.multiple_of(((place ^ s) * 2 + (core ^ piece)) * half, half)
            outs[s][piece] = result_ref[:, pl.ds(first, half), :]


def shape(*dims, dtype=jnp.bfloat16):
    return jax.ShapeDtypeStruct(dims, dtype)


def call(kernel, out_shape, *args, scratch=(), flops=0, exps=0):
    return pl.pallas_call(
        kernel,
        out_shape=out_shape,
        in_specs=[WHOLE] * len(args),
        out_specs=jax.tree.map(lambda _: WHOLE, out_shape),
        scratch_shapes=scratch,
        compiler_params=pltpu.CompilerParams(vmem_limit_bytes=VMEM),
        cost_estimate=pl.CostEstimate(flops=1, bytes_accessed=1, transcendentals=0),
    )(*args)


def pack_kernel(chunks, *refs):
    ins, outs = refs[:4], refs[4:]
    block, width = ins[0].shape
    core, place = lax.axis_index("head"), lax.axis_index("blk") % GROUP
    at = pl.ds(pl.multiple_of(pl.program_id(0) * block, block), block)
    for j in range(chunks):
        for which in range(2):
            for s in range(GROUP):
                base = (core ^ which) * (width // 2) + ((place ^ s) * chunks + j) * DH
                first = pl.multiple_of(base, DH)
                for m, ref in enumerate(ins):
                    outs[2 * j + which][s, m, at] = ref[:, pl.ds(first, DH)]


def pack(arrays, chunks):
    rows, width = arrays[0].shape
    block = rows // PACK_STEPS
    return pl.pallas_call(
        functools.partial(pack_kernel, chunks),
        grid=(PACK_STEPS,),
        out_shape=[shape(GROUP, 4, rows, DH)] * (2 * chunks),
        in_specs=[pl.BlockSpec((block, width), lambda i: (i, 0))] * 4,
        out_specs=[WHOLE] * (2 * chunks),
        compiler_params=pltpu.CompilerParams(vmem_limit_bytes=PACK_VMEM),
    )(*arrays)


def join_kernel(mine_ref, received_ref, *outs):
    for s, out in enumerate(outs):
        out[0] = mine_ref[s]
        out[1] = received_ref[s]


def gather_kernel(*refs):
    slots, (ext, to_even, to_odd) = refs[:-3], refs[-3:]
    edge = to_even.shape[1]
    half = edge // 2
    position, core = lax.axis_index("blk"), lax.axis_index("head")
    place, parity = position % GROUP, (position // GROUP) % 2
    for s, slot in zip(ORDER_IN, slots):
        for piece in range(2):
            first = pl.multiple_of(((place ^ s) * 2 + (core ^ piece)) * half, half)
            ext[:, pl.ds(first, half), :] = slot[piece]
    rows = ext.shape[1]
    first = pl.multiple_of((rows - edge) * (1 - parity), edge)
    to_even[...] = ext[:, pl.ds(first, edge), :]
    first = pl.multiple_of((rows - edge) * parity, edge)
    to_odd[...] = ext[:, pl.ds(first, edge), :]


def split_kernel(*refs):
    slots, out = refs[:-1], refs[-1]
    for s, slot in zip(ORDER_OUT, slots):
        out[s] = slot[1]


def unpack_kernel(chunks, *refs):
    ins, outs, held, sems = refs[:-6], refs[-6:-2], refs[-2], refs[-1]
    width = outs[0].shape[1]
    core, place = lax.axis_index("head"), lax.axis_index("blk") % GROUP
    blocks = []
    for j in range(chunks):
        *slots, received = ins[j * (GROUP + 1) : (j + 1) * (GROUP + 1)]
        for s, slot in zip(ORDER_OUT, slots):
            for which, block in enumerate((slot.at[0], received.at[s])):
                base = (core ^ which) * (width // 2) + ((place ^ s) * chunks + j) * DH
                blocks.append((pl.multiple_of(base, DH), block))
    copies = [pltpu.make_async_copy(held.at[m], out, sems.at[m]) for m, out in enumerate(outs)]
    for m, copy in enumerate(copies):
        for first, block in blocks:
            held[m, :, pl.ds(first, DH)] = block[m]
        copy.start()
    for copy in copies:
        copy.wait()


def unpack(chunks, rows, width):
    blocks = [block for chunk in chunks for block in chunk]
    return pl.pallas_call(
        functools.partial(unpack_kernel, len(chunks)),
        out_shape=[shape(rows, width)] * 4,
        in_specs=[WHOLE] * len(blocks),
        out_specs=[pl.BlockSpec(memory_space=pl.ANY)] * 4,
        scratch_shapes=[
            pltpu.VMEM((4, rows, width), jnp.bfloat16),
            pltpu.SemaphoreType.DMA((4,)),
        ],
        compiler_params=pltpu.CompilerParams(vmem_limit_bytes=VMEM),
    )(*blocks)


def body(query_rows, key_rows, value_rows, out_grad, doc_ids):
    positions = lax.axis_size("blk")
    half, width = query_rows.shape
    heads = width // DH
    chunks = heads // (2 * GROUP)
    edge = 2 * half
    rows = GROUP * edge
    assert edge >= DOC_MOST and positions % GROUP == 0 and chunks == 2
    swap = [(0, 1), (1, 0)]
    planes = positions // GROUP

    def plane_pairs(first):
        route = []
        for low in range(first, planes - 1, 2):
            for i in range(GROUP):
                here, there = low * GROUP + i, (low + 1) * GROUP + i
                route += [(here, there), (there, here)]
        return route

    def hop(block, s):
        return lax.ppermute(block, "blk", [(i, i ^ s) for i in range(positions)]) if s else block

    table = doc_ids.reshape(-1, half)
    inputs = (query_rows, key_rows, value_rows, out_grad)
    unit = 2 * DH * edge * edge * 6

    packed = pack(inputs, chunks)
    arrived = []
    for j in range(chunks):
        mine, other = packed[2 * j : 2 * j + 2]
        theirs = lax.ppermute(other, "head", swap)
        joined = call(join_kernel, [shape(2, 4, half, DH)] * GROUP, mine, theirs)
        arrived.append([hop(joined[s], s) for s in ORDER_IN])

    def gather(j, *after):
        slots = arrived[j]
        if after:
            slots, _ = lax.optimization_barrier((slots, after))
        return call(
            gather_kernel,
            [shape(4, rows, DH), shape(4, edge, DH), shape(4, edge, DH)],
            *slots,
        )

    def halo(to_even, to_odd):
        even = lax.ppermute(to_even, "blk", plane_pairs(0))
        return even, lax.ppermute(to_odd, "blk", plane_pairs(1))

    def interior(ext):
        return call(
            functools.partial(interior_kernel, edge), shape(4, rows, DH), ext, table
        )

    def finish(ext, even, odd, res):
        return call(
            functools.partial(edge_kernel, edge),
            [shape(2, 4, half, DH)] * GROUP,
            ext,
            even,
            odd,
            res,
            table,
            scratch=[pltpu.VMEM((4, rows, DH), jnp.bfloat16)],
        )

    def give_back(back):
        return [hop(back[s], s) for s in ORDER_OUT]

    def swap_back(back):
        away = call(split_kernel, shape(GROUP, 4, half, DH), *back)
        return back + [lax.ppermute(away, "head", swap)]

    ext_a, *edges_a = gather(0)
    halo_a = halo(*edges_a)
    res_a = interior(ext_a)
    res_a, arrived[1][1] = lax.optimization_barrier((res_a, arrived[1][1]))
    back_a = finish(ext_a, *halo_a, res_a)
    ext_b, *edges_b = gather(1, back_a)
    halo_b = halo(*edges_b)
    res_b = interior(ext_b)
    out_a = give_back(back_a)
    res_b, tied = lax.optimization_barrier((res_b, [out_a[i] for i in (1, 2)]))
    for i, block in zip((1, 2), tied):
        out_a[i] = block
    back_b = finish(ext_b, *halo_b, res_b)
    out_b = give_back(back_b)
    results = [swap_back(out_a), swap_back(out_b)]
    return tuple(unpack(results, half, width))


def solution(mesh):
    placed = P(("blk", "head"), None)
    return jax.shard_map(
        body,
        mesh=mesh,
        in_specs=(placed, placed, placed, placed, P()),
        out_specs=(placed,) * 4,
        check_vma=False,
    )
```

```python
import functools
import math

import jax
import jax.numpy as jnp
from jax import lax
from jax.experimental import pallas as pl
from jax.experimental.pallas import tpu as pltpu
from jax.sharding import PartitionSpec as P

DH = 128
DOC_MOST = 256
MASKED = -1e30
GROUP = 4
ORDER_IN = (0, 3, 2, 1)
ORDER_OUT = (0, 2, 1, 3)
SCALE = 1.0 / math.sqrt(DH)
VMEM = 12 * 1024 * 1024
PACK_VMEM = 53 * 1024 * 1024
PACK_STEPS = 2
WHOLE = pl.BlockSpec(memory_space=pltpu.VMEM)


def dot_nt(a, b):
    return lax.dot_general(a, b, (((1,), (1,)), ((), ())), preferred_element_type=jnp.float32)


def dot_tn(a, b):
    return lax.dot_general(a, b, (((0,), (0,)), ((), ())), preferred_element_type=jnp.float32)


def dot_nn(a, b):
    return lax.dot_general(a, b, (((1,), (0,)), ((), ())), preferred_element_type=jnp.float32)


def self_attention(queries, keys, values, grads, same):
    scores = dot_nt(keys, queries) * (SCALE * math.log2(math.e))
    scores = jnp.where(same, scores, jnp.float32(MASKED))
    top = jnp.max(scores, axis=0, keepdims=True)
    weights = jnp.exp2(scores - top)
    probs = weights * (1.0 / jnp.sum(weights, axis=0, keepdims=True))
    low = probs.astype(jnp.bfloat16)
    weighted = probs * dot_nt(values, grads)
    delta = jnp.sum(weighted, axis=0, keepdims=True)
    score_grad = (weighted - probs * delta).astype(jnp.bfloat16)
    attended = dot_tn(values, low).T
    query_grad = (dot_tn(keys, score_grad) * SCALE).T
    key_grad = dot_nn(score_grad, queries) * SCALE
    value_grad = dot_nn(low, grads)
    return attended, query_grad, key_grad, value_grad


def tile_ids(table_ref, first):
    lanes = []
    for row in (first, first + 1):
        inside = (row >= 0) & (row < table_ref.shape[0])
        held = jnp.clip(row, 0, table_ref.shape[0] - 1)
        lanes.append(jnp.where(inside, table_ref[pl.ds(held, 1), :], -1))
    down = [jnp.broadcast_to(lane, (lane.shape[1], lane.shape[1])).T for lane in lanes]
    return jnp.concatenate(down, axis=0), jnp.concatenate(lanes, axis=1)


def across(down):
    return jnp.concatenate([down, down], axis=1)


def boundary_attention(low_rows, high_rows, ids_low, ids_high):
    (low_down, low_lane), (high_down, high_lane) = ids_low, ids_high
    first, last = high_lane[:, 0:1], low_lane[:, -1:]
    from_low, from_high = low_down == first, high_down == last
    member_down = (from_low | from_high).astype(jnp.int32)
    member_lane = ((low_lane == first) | (high_lane == last)).astype(jnp.int32)
    chosen = [
        jnp.where(from_low, a.astype(jnp.float32), b.astype(jnp.float32)).astype(jnp.bfloat16)
        for a, b in zip(low_rows, high_rows)
    ]
    return self_attention(*chosen, across(member_down) == member_lane), from_low, from_high


def interior_kernel(edge, ext_ref, table_ref, res_ref):
    tiles = ext_ref.shape[1] // edge
    plane = lax.axis_index("blk") // GROUP
    ids = [tile_ids(table_ref, (plane * tiles + t) * 2) for t in range(tiles)]

    def rows_of(t):
        return [ext_ref[m, t * edge : (t + 1) * edge] for m in range(4)]

    def put(t, chosen, results):
        at = slice(t * edge, (t + 1) * edge)
        for m, result in enumerate(results):
            if chosen is not None:
                result = jnp.where(chosen, result, res_ref[m, at].astype(jnp.float32))
            res_ref[m, at] = result.astype(jnp.bfloat16)

    for t in range(tiles):
        down, lane = ids[t]
        put(t, None, self_attention(*rows_of(t), across(down) == lane))
        if t > 0:
            results, from_low, from_high = boundary_attention(
                rows_of(t - 1), rows_of(t), ids[t - 1], ids[t]
            )
            put(t - 1, from_low, results)
            put(t, from_high, results)


def edge_kernel(edge, ext_ref, even_ref, odd_ref, res_ref, table_ref, *refs):
    outs, result_ref = refs[:-1], refs[-1]
    rows = ext_ref.shape[1]
    position, core = lax.axis_index("blk"), lax.axis_index("head")
    place, parity = position % GROUP, (position // GROUP) % 2
    tiles = rows // edge
    base = (position // GROUP) * tiles
    ends = []

    for side in range(2):
        from_even = parity == (1 - side)
        halo = [jnp.where(from_even, even_ref[m], odd_ref[m]) for m in range(4)]
        own = slice(0, edge) if side == 0 else slice(rows - edge, rows)
        mine = [ext_ref[m, own] for m in range(4)]
        if side == 0:
            results, _, chosen = boundary_attention(
                halo, mine, tile_ids(table_ref, (base - 1) * 2), tile_ids(table_ref, base * 2)
            )
        else:
            results, chosen, _ = boundary_attention(
                mine,
                halo,
                tile_ids(table_ref, (base + tiles - 1) * 2),
                tile_ids(table_ref, (base + tiles) * 2),
            )
        ends.append((own, results, chosen))
    result_ref[:, edge : rows - edge] = res_ref[:, edge : rows - edge]
    for own, results, chosen in ends:
        for m, result in enumerate(results):
            result = jnp.where(chosen, result, res_ref[m, own].astype(jnp.float32))
            result_ref[m, own] = result.astype(jnp.bfloat16)
    half = edge // 2
    for s in range(GROUP):
        for piece in range(2):
            first = pl.multiple_of(((place ^ s) * 2 + (core ^ piece)) * half, half)
            outs[s][piece] = result_ref[:, pl.ds(first, half), :]


def shape(*dims, dtype=jnp.bfloat16):
    return jax.ShapeDtypeStruct(dims, dtype)


def call(kernel, out_shape, *args, scratch=(), flops=0, exps=0):
    return pl.pallas_call(
        kernel,
        out_shape=out_shape,
        in_specs=[WHOLE] * len(args),
        out_specs=jax.tree.map(lambda _: WHOLE, out_shape),
        scratch_shapes=scratch,
        compiler_params=pltpu.CompilerParams(vmem_limit_bytes=VMEM),
    )(*args)


def pack_kernel(chunks, *refs):
    ins, outs = refs[:4], refs[4:]
    block, width = ins[0].shape
    core, place = lax.axis_index("head"), lax.axis_index("blk") % GROUP
    at = pl.ds(pl.multiple_of(pl.program_id(0) * block, block), block)
    for j in range(chunks):
        for which in range(2):
            for s in range(GROUP):
                base = (core ^ which) * (width // 2) + ((place ^ s) * chunks + j) * DH
                first = pl.multiple_of(base, DH)
                for m, ref in enumerate(ins):
                    outs[2 * j + which][s, m, at] = ref[:, pl.ds(first, DH)]


def pack(arrays, chunks):
    rows, width = arrays[0].shape
    block = rows // PACK_STEPS
    return pl.pallas_call(
        functools.partial(pack_kernel, chunks),
        grid=(PACK_STEPS,),
        out_shape=[shape(GROUP, 4, rows, DH)] * (2 * chunks),
        in_specs=[pl.BlockSpec((block, width), lambda i: (i, 0))] * 4,
        out_specs=[WHOLE] * (2 * chunks),
        compiler_params=pltpu.CompilerParams(vmem_limit_bytes=PACK_VMEM),
    )(*arrays)


def join_kernel(mine_ref, received_ref, *outs):
    for s, out in enumerate(outs):
        out[0] = mine_ref[s]
        out[1] = received_ref[s]


def gather_kernel(*refs):
    slots, (ext, to_even, to_odd) = refs[:-3], refs[-3:]
    edge = to_even.shape[1]
    half = edge // 2
    position, core = lax.axis_index("blk"), lax.axis_index("head")
    place, parity = position % GROUP, (position // GROUP) % 2
    for s, slot in zip(ORDER_IN, slots):
        for piece in range(2):
            first = pl.multiple_of(((place ^ s) * 2 + (core ^ piece)) * half, half)
            ext[:, pl.ds(first, half), :] = slot[piece]
    rows = ext.shape[1]
    first = pl.multiple_of((rows - edge) * (1 - parity), edge)
    to_even[...] = ext[:, pl.ds(first, edge), :]
    first = pl.multiple_of((rows - edge) * parity, edge)
    to_odd[...] = ext[:, pl.ds(first, edge), :]


def split_kernel(*refs):
    slots, out = refs[:-1], refs[-1]
    for s, slot in zip(ORDER_OUT, slots):
        out[s] = slot[1]


def unpack_kernel(chunks, *refs):
    ins, outs, held, sems = refs[:-6], refs[-6:-2], refs[-2], refs[-1]
    width = outs[0].shape[1]
    core, place = lax.axis_index("head"), lax.axis_index("blk") % GROUP
    blocks = []
    for j in range(chunks):
        *slots, received = ins[j * (GROUP + 1) : (j + 1) * (GROUP + 1)]
        for s, slot in zip(ORDER_OUT, slots):
            for which, block in enumerate((slot.at[0], received.at[s])):
                base = (core ^ which) * (width // 2) + ((place ^ s) * chunks + j) * DH
                blocks.append((pl.multiple_of(base, DH), block))
    rows = held.shape[1]
    parts = sems.shape[1]
    copies = []
    for m, out in enumerate(outs):
        for i in range(parts):
            at = slice(i * rows // parts, (i + 1) * rows // parts)
            for first, block in blocks:
                held[m, at, pl.ds(first, DH)] = block[m, at]
            copies.append(pltpu.make_async_copy(held.at[m, at], out.at[at], sems.at[m, i]))
            copies[-1].start()
    for copy in copies:
        copy.wait()


def unpack(chunks, rows, width):
    blocks = [block for chunk in chunks for block in chunk]
    return pl.pallas_call(
        functools.partial(unpack_kernel, len(chunks)),
        out_shape=[shape(rows, width)] * 4,
        in_specs=[WHOLE] * len(blocks),
        out_specs=[pl.BlockSpec(memory_space=pl.ANY)] * 4,
        scratch_shapes=[
            pltpu.VMEM((4, rows, width), jnp.bfloat16),
            pltpu.SemaphoreType.DMA((4, 2)),
        ],
        compiler_params=pltpu.CompilerParams(vmem_limit_bytes=VMEM),
    )(*blocks)


def body(query_rows, key_rows, value_rows, out_grad, doc_ids):
    positions = lax.axis_size("blk")
    half, width = query_rows.shape
    heads = width // DH
    chunks = heads // (2 * GROUP)
    edge = 2 * half
    rows = GROUP * edge
    assert edge >= DOC_MOST and positions % GROUP == 0 and chunks == 2
    swap = [(0, 1), (1, 0)]
    planes = positions // GROUP

    def plane_pairs(first):
        route = []
        for low in range(first, planes - 1, 2):
            for i in range(GROUP):
                here, there = low * GROUP + i, (low + 1) * GROUP + i
                route += [(here, there), (there, here)]
        return route

    def hop(block, s):
        return lax.ppermute(block, "blk", [(i, i ^ s) for i in range(positions)]) if s else block

    table = doc_ids.reshape(-1, half)
    inputs = (query_rows, key_rows, value_rows, out_grad)
    unit = 2 * DH * edge * edge * 6

    packed = pack(inputs, chunks)
    arrived = []
    for j in range(chunks):
        mine, other = packed[2 * j : 2 * j + 2]
        theirs = lax.ppermute(other, "head", swap)
        joined = call(join_kernel, [shape(2, 4, half, DH)] * GROUP, mine, theirs)
        arrived.append([hop(joined[s], s) for s in ORDER_IN])

    def gather(j, *after):
        slots = arrived[j]
        if after:
            slots, _ = lax.optimization_barrier((slots, after))
        return call(
            gather_kernel,
            [shape(4, rows, DH), shape(4, edge, DH), shape(4, edge, DH)],
            *slots,
        )

    def halo(to_even, to_odd):
        even = lax.ppermute(to_even, "blk", plane_pairs(0))
        return even, lax.ppermute(to_odd, "blk", plane_pairs(1))

    def interior(ext):
        return call(
            functools.partial(interior_kernel, edge), shape(4, rows, DH), ext, table
        )

    def finish(ext, even, odd, res):
        return call(
            functools.partial(edge_kernel, edge),
            [shape(2, 4, half, DH)] * GROUP,
            ext,
            even,
            odd,
            res,
            table,
            scratch=[pltpu.VMEM((4, rows, DH), jnp.bfloat16)],
        )

    def give_back(back):
        return [hop(back[s], s) for s in ORDER_OUT]

    def swap_back(back):
        away = call(split_kernel, shape(GROUP, 4, half, DH), *back)
        return back + [lax.ppermute(away, "head", swap)]

    ext_a, *edges_a = gather(0)
    halo_a = halo(*edges_a)
    res_a = interior(ext_a)
    res_a, arrived[1][1] = lax.optimization_barrier((res_a, arrived[1][1]))
    back_a = finish(ext_a, *halo_a, res_a)
    ext_b, *edges_b = gather(1, back_a)
    halo_b = halo(*edges_b)
    res_b = interior(ext_b)
    out_a = give_back(back_a)
    res_b, tied = lax.optimization_barrier((res_b, [out_a[i] for i in (1, 2)]))
    for i, block in zip((1, 2), tied):
        out_a[i] = block
    back_b = finish(ext_b, *halo_b, res_b)
    out_b = give_back(back_b)
    results = [swap_back(out_a), swap_back(out_b)]
    return tuple(unpack(results, half, width))


def solution(mesh):
    placed = P(("blk", "head"), None)
    return jax.shard_map(
        body,
        mesh=mesh,
        in_specs=(placed, placed, placed, placed, P()),
        out_specs=(placed,) * 4,
        check_vma=False,
    )
```

```python
import functools
import math

import jax
import jax.numpy as jnp
from jax import lax
from jax.experimental import pallas as pl
from jax.experimental.pallas import tpu as pltpu
from jax.sharding import PartitionSpec as P

DH = 128
DOC_MOST = 256
MASKED = -1e30
GROUP = 4
ORDER_IN = (0, 3, 2, 1)
ORDER_OUT = (0, 2, 1, 3)
SCALE = 1.0 / math.sqrt(DH)
VMEM = 12 * 1024 * 1024
PACK_VMEM = 53 * 1024 * 1024
PACK_STEPS = 1
WHOLE = pl.BlockSpec(memory_space=pltpu.VMEM)


def dot_nt(a, b):
    return lax.dot_general(a, b, (((1,), (1,)), ((), ())), preferred_element_type=jnp.float32)


def dot_tn(a, b):
    return lax.dot_general(a, b, (((0,), (0,)), ((), ())), preferred_element_type=jnp.float32)


def dot_nn(a, b):
    return lax.dot_general(a, b, (((1,), (0,)), ((), ())), preferred_element_type=jnp.float32)


def self_attention(queries, keys, values, grads, same):
    scores = dot_nt(keys, queries) * (SCALE * math.log2(math.e))
    scores = jnp.where(same, scores, jnp.float32(MASKED))
    top = jnp.max(scores, axis=0, keepdims=True)
    weights = jnp.exp2(scores - top)
    probs = weights * (1.0 / jnp.sum(weights, axis=0, keepdims=True))
    low = probs.astype(jnp.bfloat16)
    weighted = probs * dot_nt(values, grads)
    delta = jnp.sum(weighted, axis=0, keepdims=True)
    score_grad = (weighted - probs * delta).astype(jnp.bfloat16)
    attended = dot_tn(values, low).T
    query_grad = (dot_tn(keys, score_grad) * SCALE).T
    key_grad = dot_nn(score_grad, queries) * SCALE
    value_grad = dot_nn(low, grads)
    return attended, query_grad, key_grad, value_grad


def tile_ids(table_ref, first):
    lanes = []
    for row in (first, first + 1):
        inside = (row >= 0) & (row < table_ref.shape[0])
        held = jnp.clip(row, 0, table_ref.shape[0] - 1)
        lanes.append(jnp.where(inside, table_ref[pl.ds(held, 1), :], -1))
    down = [jnp.broadcast_to(lane, (lane.shape[1], lane.shape[1])).T for lane in lanes]
    return jnp.concatenate(down, axis=0), jnp.concatenate(lanes, axis=1)


def across(down):
    return jnp.concatenate([down, down], axis=1)


def boundary_attention(low_rows, high_rows, ids_low, ids_high):
    (low_down, low_lane), (high_down, high_lane) = ids_low, ids_high
    first, last = high_lane[:, 0:1], low_lane[:, -1:]
    from_low, from_high = low_down == first, high_down == last
    member_down = (from_low | from_high).astype(jnp.int32)
    member_lane = ((low_lane == first) | (high_lane == last)).astype(jnp.int32)
    chosen = [
        jnp.where(from_low, a.astype(jnp.float32), b.astype(jnp.float32)).astype(jnp.bfloat16)
        for a, b in zip(low_rows, high_rows)
    ]
    return self_attention(*chosen, across(member_down) == member_lane), from_low, from_high


def interior_kernel(edge, ext_ref, table_ref, res_ref):
    tiles = ext_ref.shape[1] // edge
    plane = lax.axis_index("blk") // GROUP
    ids = [tile_ids(table_ref, (plane * tiles + t) * 2) for t in range(tiles)]

    def rows_of(t):
        return [ext_ref[m, t * edge : (t + 1) * edge] for m in range(4)]

    def put(t, chosen, results):
        at = slice(t * edge, (t + 1) * edge)
        for m, result in enumerate(results):
            if chosen is not None:
                result = jnp.where(chosen, result, res_ref[m, at].astype(jnp.float32))
            res_ref[m, at] = result.astype(jnp.bfloat16)

    for t in range(tiles):
        down, lane = ids[t]
        put(t, None, self_attention(*rows_of(t), across(down) == lane))
        if t > 0:
            results, from_low, from_high = boundary_attention(
                rows_of(t - 1), rows_of(t), ids[t - 1], ids[t]
            )
            put(t - 1, from_low, results)
            put(t, from_high, results)


def edge_kernel(edge, ext_ref, even_ref, odd_ref, res_ref, table_ref, *refs):
    outs, result_ref = refs[:-1], refs[-1]
    rows = ext_ref.shape[1]
    position, core = lax.axis_index("blk"), lax.axis_index("head")
    place, parity = position % GROUP, (position // GROUP) % 2
    tiles = rows // edge
    base = (position // GROUP) * tiles
    ends = []

    for side in range(2):
        from_even = parity == (1 - side)
        halo = [jnp.where(from_even, even_ref[m], odd_ref[m]) for m in range(4)]
        own = slice(0, edge) if side == 0 else slice(rows - edge, rows)
        mine = [ext_ref[m, own] for m in range(4)]
        if side == 0:
            results, _, chosen = boundary_attention(
                halo, mine, tile_ids(table_ref, (base - 1) * 2), tile_ids(table_ref, base * 2)
            )
        else:
            results, chosen, _ = boundary_attention(
                mine,
                halo,
                tile_ids(table_ref, (base + tiles - 1) * 2),
                tile_ids(table_ref, (base + tiles) * 2),
            )
        ends.append((own, results, chosen))
    result_ref[:, edge : rows - edge] = res_ref[:, edge : rows - edge]
    for own, results, chosen in ends:
        for m, result in enumerate(results):
            result = jnp.where(chosen, result, res_ref[m, own].astype(jnp.float32))
            result_ref[m, own] = result.astype(jnp.bfloat16)
    half = edge // 2
    for s in range(GROUP):
        for piece in range(2):
            first = pl.multiple_of(((place ^ s) * 2 + (core ^ piece)) * half, half)
            outs[s][piece] = result_ref[:, pl.ds(first, half), :]


def shape(*dims, dtype=jnp.bfloat16):
    return jax.ShapeDtypeStruct(dims, dtype)


def call(kernel, out_shape, *args, scratch=(), flops=0, exps=0):
    return pl.pallas_call(
        kernel,
        out_shape=out_shape,
        in_specs=[WHOLE] * len(args),
        out_specs=jax.tree.map(lambda _: WHOLE, out_shape),
        scratch_shapes=scratch,
        compiler_params=pltpu.CompilerParams(vmem_limit_bytes=VMEM),
    )(*args)


def pack_kernel(chunks, core_ref, *refs):
    ins, outs = refs[:4], refs[4:]
    block = ins[0].shape[0]
    place = lax.axis_index("blk") % GROUP
    at = pl.ds(pl.multiple_of(pl.program_id(0) * block, block), block)
    for j in range(chunks):
        for s in range(GROUP):
            first = pl.multiple_of(((place ^ s) * chunks + j) * DH, DH)
            for m, ref in enumerate(ins):
                outs[j][s, m, at] = ref[:, pl.ds(first, DH)]


def pack(arrays, chunks, core):
    rows, width = arrays[0].shape
    block = rows // PACK_STEPS
    return pl.pallas_call(
        functools.partial(pack_kernel, chunks),
        grid_spec=pltpu.PrefetchScalarGridSpec(
            num_scalar_prefetch=1,
            grid=(PACK_STEPS,),
            in_specs=[pl.BlockSpec((block, width // 2), lambda i, core: (i, core[0]))] * 4,
            out_specs=[WHOLE] * chunks,
        ),
        out_shape=[shape(GROUP, 4, rows, DH)] * chunks,
        compiler_params=pltpu.CompilerParams(vmem_limit_bytes=PACK_VMEM),
    )(core, *arrays)


def join_kernel(mine_ref, received_ref, *outs):
    for s, out in enumerate(outs):
        out[0] = mine_ref[s]
        out[1] = received_ref[s]


def gather_kernel(*refs):
    slots, (ext, to_even, to_odd) = refs[:-3], refs[-3:]
    edge = to_even.shape[1]
    half = edge // 2
    position, core = lax.axis_index("blk"), lax.axis_index("head")
    place, parity = position % GROUP, (position // GROUP) % 2
    for s, slot in zip(ORDER_IN, slots):
        for piece in range(2):
            first = pl.multiple_of(((place ^ s) * 2 + (core ^ piece)) * half, half)
            ext[:, pl.ds(first, half), :] = slot[piece]
    rows = ext.shape[1]
    first = pl.multiple_of((rows - edge) * (1 - parity), edge)
    to_even[...] = ext[:, pl.ds(first, edge), :]
    first = pl.multiple_of((rows - edge) * parity, edge)
    to_odd[...] = ext[:, pl.ds(first, edge), :]


def split_kernel(*refs):
    slots, out = refs[:-1], refs[-1]
    for s, slot in zip(ORDER_OUT, slots):
        out[s] = slot[1]


def unpack_kernel(chunks, *refs):
    ins, outs, held, sems = refs[:-6], refs[-6:-2], refs[-2], refs[-1]
    width = outs[0].shape[1]
    core, place = lax.axis_index("head"), lax.axis_index("blk") % GROUP
    blocks = []
    for j in range(chunks):
        *slots, received = ins[j * (GROUP + 1) : (j + 1) * (GROUP + 1)]
        for s, slot in zip(ORDER_OUT, slots):
            for which, block in enumerate((slot.at[0], received.at[s])):
                base = (core ^ which) * (width // 2) + ((place ^ s) * chunks + j) * DH
                blocks.append((pl.multiple_of(base, DH), block))
    rows = held.shape[1]
    parts = sems.shape[1]
    copies = []
    for m, out in enumerate(outs):
        for i in range(parts):
            at = slice(i * rows // parts, (i + 1) * rows // parts)
            for first, block in blocks:
                held[m, at, pl.ds(first, DH)] = block[m, at]
            copies.append(pltpu.make_async_copy(held.at[m, at], out.at[at], sems.at[m, i]))
            copies[-1].start()
    for copy in copies:
        copy.wait()


def unpack(chunks, rows, width):
    blocks = [block for chunk in chunks for block in chunk]
    return pl.pallas_call(
        functools.partial(unpack_kernel, len(chunks)),
        out_shape=[shape(rows, width)] * 4,
        in_specs=[WHOLE] * len(blocks),
        out_specs=[pl.BlockSpec(memory_space=pl.ANY)] * 4,
        scratch_shapes=[
            pltpu.VMEM((4, rows, width), jnp.bfloat16),
            pltpu.SemaphoreType.DMA((4, 2)),
        ],
        compiler_params=pltpu.CompilerParams(vmem_limit_bytes=VMEM),
    )(*blocks)


def body(query_rows, key_rows, value_rows, out_grad, doc_ids):
    positions = lax.axis_size("blk")
    half, width = query_rows.shape
    heads = width // DH
    chunks = heads // (2 * GROUP)
    edge = 2 * half
    rows = GROUP * edge
    assert edge >= DOC_MOST and positions % GROUP == 0 and chunks == 2
    swap = [(0, 1), (1, 0)]
    planes = positions // GROUP

    def plane_pairs(first):
        route = []
        for low in range(first, planes - 1, 2):
            for i in range(GROUP):
                here, there = low * GROUP + i, (low + 1) * GROUP + i
                route += [(here, there), (there, here)]
        return route

    def hop(block, s):
        return lax.ppermute(block, "blk", [(i, i ^ s) for i in range(positions)]) if s else block

    table = doc_ids.reshape(-1, half)
    inputs = (query_rows, key_rows, value_rows, out_grad)
    unit = 2 * DH * edge * edge * 6

    core = lax.axis_index("head").reshape(1)
    others = pack(inputs, chunks, 1 - core)
    own = pack(inputs, chunks, core)
    arrived = []
    for j in range(chunks):
        mine, other = own[j], others[j]
        theirs = lax.ppermute(other, "head", swap)
        joined = call(join_kernel, [shape(2, 4, half, DH)] * GROUP, mine, theirs)
        arrived.append([hop(joined[s], s) for s in ORDER_IN])

    def gather(j, *after):
        slots = arrived[j]
        if after:
            slots, _ = lax.optimization_barrier((slots, after))
        return call(
            gather_kernel,
            [shape(4, rows, DH), shape(4, edge, DH), shape(4, edge, DH)],
            *slots,
        )

    def halo(to_even, to_odd):
        even = lax.ppermute(to_even, "blk", plane_pairs(0))
        return even, lax.ppermute(to_odd, "blk", plane_pairs(1))

    def interior(ext):
        return call(
            functools.partial(interior_kernel, edge), shape(4, rows, DH), ext, table
        )

    def finish(ext, even, odd, res):
        return call(
            functools.partial(edge_kernel, edge),
            [shape(2, 4, half, DH)] * GROUP,
            ext,
            even,
            odd,
            res,
            table,
            scratch=[pltpu.VMEM((4, rows, DH), jnp.bfloat16)],
        )

    def give_back(back):
        return [hop(back[s], s) for s in ORDER_OUT]

    def swap_back(back):
        away = call(split_kernel, shape(GROUP, 4, half, DH), *back)
        return back + [lax.ppermute(away, "head", swap)]

    ext_a, *edges_a = gather(0)
    halo_a = halo(*edges_a)
    res_a = interior(ext_a)
    res_a, arrived[1][1] = lax.optimization_barrier((res_a, arrived[1][1]))
    back_a = finish(ext_a, *halo_a, res_a)
    ext_b, *edges_b = gather(1, back_a)
    halo_b = halo(*edges_b)
    res_b = interior(ext_b)
    out_a = give_back(back_a)
    res_b, tied = lax.optimization_barrier((res_b, [out_a[i] for i in (1, 2)]))
    for i, block in zip((1, 2), tied):
        out_a[i] = block
    back_b = finish(ext_b, *halo_b, res_b)
    out_b = give_back(back_b)
    results = [swap_back(out_a), swap_back(out_b)]
    return tuple(unpack(results, half, width))


def solution(mesh):
    placed = P(("blk", "head"), None)
    return jax.shard_map(
        body,
        mesh=mesh,
        in_specs=(placed, placed, placed, placed, P()),
        out_specs=(placed,) * 4,
        check_vma=False,
    )
```

```python
import functools
import math

import jax
import jax.numpy as jnp
from jax import lax
from jax.experimental import pallas as pl
from jax.experimental.pallas import tpu as pltpu
from jax.sharding import PartitionSpec as P

DH = 128
DOC_MOST = 256
MASKED = -1e30
GROUP = 4
ORDER_IN = (0, 3, 2, 1)
ORDER_OUT = (0, 2, 1, 3)
SCALE = 1.0 / math.sqrt(DH)
VMEM = 20 * 1024 * 1024
PACK_VMEM = 53 * 1024 * 1024
PACK_STEPS = 2
WHOLE = pl.BlockSpec(memory_space=pltpu.VMEM)


def dot_nt(a, b):
    return lax.dot_general(a, b, (((1,), (1,)), ((), ())), preferred_element_type=jnp.float32)


def dot_tn(a, b):
    return lax.dot_general(a, b, (((0,), (0,)), ((), ())), preferred_element_type=jnp.float32)


def dot_nn(a, b):
    return lax.dot_general(a, b, (((1,), (0,)), ((), ())), preferred_element_type=jnp.float32)


def self_attention(queries, keys, values, grads, same):
    scores = dot_nt(keys, queries) * (SCALE * math.log2(math.e))
    scores = jnp.where(same, scores, jnp.float32(MASKED))
    top = jnp.max(scores, axis=0, keepdims=True)
    weights = jnp.exp2(scores - top)
    probs = weights * (1.0 / jnp.sum(weights, axis=0, keepdims=True))
    low = probs.astype(jnp.bfloat16)
    weighted = probs * dot_nt(values, grads)
    delta = jnp.sum(weighted, axis=0, keepdims=True)
    score_grad = (weighted - probs * delta).astype(jnp.bfloat16)
    attended = dot_tn(values, low).T
    query_grad = (dot_tn(keys, score_grad) * SCALE).T
    key_grad = dot_nn(score_grad, queries) * SCALE
    value_grad = dot_nn(low, grads)
    return attended, query_grad, key_grad, value_grad


def tile_ids(table_ref, first):
    lanes = []
    for row in (first, first + 1):
        inside = (row >= 0) & (row < table_ref.shape[0])
        held = jnp.clip(row, 0, table_ref.shape[0] - 1)
        lanes.append(jnp.where(inside, table_ref[pl.ds(held, 1), :], -1))
    down = [jnp.broadcast_to(lane, (lane.shape[1], lane.shape[1])).T for lane in lanes]
    return jnp.concatenate(down, axis=0), jnp.concatenate(lanes, axis=1)


def across(down):
    return jnp.concatenate([down, down], axis=1)


def boundary_attention(low_rows, high_rows, ids_low, ids_high):
    (low_down, low_lane), (high_down, high_lane) = ids_low, ids_high
    first, last = high_lane[:, 0:1], low_lane[:, -1:]
    from_low, from_high = low_down == first, high_down == last
    member_down = (from_low | from_high).astype(jnp.int32)
    member_lane = ((low_lane == first) | (high_lane == last)).astype(jnp.int32)
    chosen = [
        jnp.where(from_low, a.astype(jnp.float32), b.astype(jnp.float32)).astype(jnp.bfloat16)
        for a, b in zip(low_rows, high_rows)
    ]
    return self_attention(*chosen, across(member_down) == member_lane), from_low, from_high


def interior_kernel(edge, ext_ref, table_ref, res_ref):
    tiles = ext_ref.shape[1] // edge
    plane = lax.axis_index("blk") // GROUP
    ids = [tile_ids(table_ref, (plane * tiles + t) * 2) for t in range(tiles)]

    def rows_of(t):
        return [ext_ref[m, t * edge : (t + 1) * edge] for m in range(4)]

    def put(t, chosen, results):
        at = slice(t * edge, (t + 1) * edge)
        for m, result in enumerate(results):
            if chosen is not None:
                result = jnp.where(chosen, result, res_ref[m, at].astype(jnp.float32))
            res_ref[m, at] = result.astype(jnp.bfloat16)

    for t in range(tiles):
        down, lane = ids[t]
        put(t, None, self_attention(*rows_of(t), across(down) == lane))
        if t > 0:
            results, from_low, from_high = boundary_attention(
                rows_of(t - 1), rows_of(t), ids[t - 1], ids[t]
            )
            put(t - 1, from_low, results)
            put(t, from_high, results)


def edge_kernel(edge, ext_ref, even_ref, odd_ref, res_ref, table_ref, *refs):
    outs, result_ref = refs[:-1], refs[-1]
    rows = ext_ref.shape[1]
    position, core = lax.axis_index("blk"), lax.axis_index("head")
    place, parity = position % GROUP, (position // GROUP) % 2
    tiles = rows // edge
    base = (position // GROUP) * tiles
    ends = []

    for side in range(2):
        from_even = parity == (1 - side)
        halo = [jnp.where(from_even, even_ref[m], odd_ref[m]) for m in range(4)]
        own = slice(0, edge) if side == 0 else slice(rows - edge, rows)
        mine = [ext_ref[m, own] for m in range(4)]
        if side == 0:
            results, _, chosen = boundary_attention(
                halo, mine, tile_ids(table_ref, (base - 1) * 2), tile_ids(table_ref, base * 2)
            )
        else:
            results, chosen, _ = boundary_attention(
                mine,
                halo,
                tile_ids(table_ref, (base + tiles - 1) * 2),
                tile_ids(table_ref, (base + tiles) * 2),
            )
        ends.append((own, results, chosen))
    result_ref[:, edge : rows - edge] = res_ref[:, edge : rows - edge]
    for own, results, chosen in ends:
        for m, result in enumerate(results):
            result = jnp.where(chosen, result, res_ref[m, own].astype(jnp.float32))
            result_ref[m, own] = result.astype(jnp.bfloat16)
    half = edge // 2
    for s in range(GROUP):
        for piece in range(2):
            first = pl.multiple_of(((place ^ s) * 2 + (core ^ piece)) * half, half)
            outs[s][piece] = result_ref[:, pl.ds(first, half), :]


def shape(*dims, dtype=jnp.bfloat16):
    return jax.ShapeDtypeStruct(dims, dtype)


def call(kernel, out_shape, *args, scratch=(), flops=0, exps=0):
    return pl.pallas_call(
        kernel,
        out_shape=out_shape,
        in_specs=[WHOLE] * len(args),
        out_specs=jax.tree.map(lambda _: WHOLE, out_shape),
        scratch_shapes=scratch,
        compiler_params=pltpu.CompilerParams(vmem_limit_bytes=VMEM),
    )(*args)


def pack_kernel(chunks, *refs):
    ins, outs = refs[:4], refs[4:]
    block, width = ins[0].shape
    core, place = lax.axis_index("head"), lax.axis_index("blk") % GROUP
    at = pl.ds(pl.multiple_of(pl.program_id(0) * block, block), block)
    for j in range(chunks):
        for which in range(2):
            for s in range(GROUP):
                base = (core ^ which) * (width // 2) + ((place ^ s) * chunks + j) * DH
                first = pl.multiple_of(base, DH)
                for m, ref in enumerate(ins):
                    outs[2 * j + which][s, m, at] = ref[:, pl.ds(first, DH)]


def pack(arrays, chunks):
    rows, width = arrays[0].shape
    block = rows // PACK_STEPS
    return pl.pallas_call(
        functools.partial(pack_kernel, chunks),
        grid=(PACK_STEPS,),
        out_shape=[shape(GROUP, 4, rows, DH)] * (2 * chunks),
        in_specs=[pl.BlockSpec((block, width), lambda i: (i, 0))] * 4,
        out_specs=[WHOLE] * (2 * chunks),
        compiler_params=pltpu.CompilerParams(vmem_limit_bytes=PACK_VMEM),
    )(*arrays)


def join_kernel(mine_ref, received_ref, *outs):
    for s, out in enumerate(outs):
        out[0] = mine_ref[s]
        out[1] = received_ref[s]


def gather_kernel(*refs):
    slots, (ext, to_even, to_odd) = refs[:-3], refs[-3:]
    edge = to_even.shape[1]
    half = edge // 2
    position, core = lax.axis_index("blk"), lax.axis_index("head")
    place, parity = position % GROUP, (position // GROUP) % 2
    for s, slot in zip(ORDER_IN, slots):
        for piece in range(2):
            first = pl.multiple_of(((place ^ s) * 2 + (core ^ piece)) * half, half)
            ext[:, pl.ds(first, half), :] = slot[piece]
    rows = ext.shape[1]
    first = pl.multiple_of((rows - edge) * (1 - parity), edge)
    to_even[...] = ext[:, pl.ds(first, edge), :]
    first = pl.multiple_of((rows - edge) * parity, edge)
    to_odd[...] = ext[:, pl.ds(first, edge), :]


def split_kernel(*refs):
    slots, out = refs[:-1], refs[-1]
    for s, slot in zip(ORDER_OUT, slots):
        out[s] = slot[1]


def unpack_kernel(chunks, *refs):
    ins, outs, held, sems = refs[:-6], refs[-6:-2], refs[-2], refs[-1]
    width = outs[0].shape[1]
    core, place = lax.axis_index("head"), lax.axis_index("blk") % GROUP
    blocks = []
    for j in range(chunks):
        *slots, received = ins[j * (GROUP + 1) : (j + 1) * (GROUP + 1)]
        for s, slot in zip(ORDER_OUT, slots):
            for which, block in enumerate((slot.at[0], received.at[s])):
                base = (core ^ which) * (width // 2) + ((place ^ s) * chunks + j) * DH
                blocks.append((pl.multiple_of(base, DH), block))
    rows = held.shape[1]
    parts = sems.shape[1]
    copies = []
    for m, out in enumerate(outs):
        for i in range(parts):
            at = slice(i * rows // parts, (i + 1) * rows // parts)
            for first, block in blocks:
                held[m, at, pl.ds(first, DH)] = block[m, at]
            copies.append(pltpu.make_async_copy(held.at[m, at], out.at[at], sems.at[m, i]))
            copies[-1].start()
    for copy in copies:
        copy.wait()


def unpack(chunks, rows, width):
    blocks = [block for chunk in chunks for block in chunk]
    return pl.pallas_call(
        functools.partial(unpack_kernel, len(chunks)),
        out_shape=[shape(rows, width)] * 4,
        in_specs=[WHOLE] * len(blocks),
        out_specs=[pl.BlockSpec(memory_space=pl.ANY)] * 4,
        scratch_shapes=[
            pltpu.VMEM((4, rows, width), jnp.bfloat16),
            pltpu.SemaphoreType.DMA((4, 2)),
        ],
        compiler_params=pltpu.CompilerParams(vmem_limit_bytes=VMEM),
    )(*blocks)


def body(query_rows, key_rows, value_rows, out_grad, doc_ids):
    positions = lax.axis_size("blk")
    half, width = query_rows.shape
    heads = width // DH
    chunks = heads // (2 * GROUP)
    edge = 2 * half
    rows = GROUP * edge
    assert edge >= DOC_MOST and positions % GROUP == 0 and chunks == 2
    swap = [(0, 1), (1, 0)]
    planes = positions // GROUP

    def plane_pairs(first):
        route = []
        for low in range(first, planes - 1, 2):
            for i in range(GROUP):
                here, there = low * GROUP + i, (low + 1) * GROUP + i
                route += [(here, there), (there, here)]
        return route

    def hop(block, s):
        return lax.ppermute(block, "blk", [(i, i ^ s) for i in range(positions)]) if s else block

    table = doc_ids.reshape(-1, half)
    inputs = (query_rows, key_rows, value_rows, out_grad)
    unit = 2 * DH * edge * edge * 6

    packed = pack(inputs, chunks)
    arrived = []
    for j in range(chunks):
        mine, other = packed[2 * j : 2 * j + 2]
        theirs = lax.ppermute(other, "head", swap)
        joined = call(join_kernel, [shape(2, 4, half, DH)] * GROUP, mine, theirs)
        arrived.append([hop(joined[s], s) for s in ORDER_IN])

    def gather(j, *after):
        slots = arrived[j]
        if after:
            slots, _ = lax.optimization_barrier((slots, after))
        return call(
            gather_kernel,
            [shape(4, rows, DH), shape(4, edge, DH), shape(4, edge, DH)],
            *slots,
        )

    def halo(to_even, to_odd):
        even = lax.ppermute(to_even, "blk", plane_pairs(0))
        return even, lax.ppermute(to_odd, "blk", plane_pairs(1))

    def interior(ext):
        return call(
            functools.partial(interior_kernel, edge), shape(4, rows, DH), ext, table
        )

    def finish(ext, even, odd, res):
        return call(
            functools.partial(edge_kernel, edge),
            [shape(2, 4, half, DH)] * GROUP,
            ext,
            even,
            odd,
            res,
            table,
            scratch=[pltpu.VMEM((4, rows, DH), jnp.bfloat16)],
        )

    def give_back(back):
        return [hop(back[s], s) for s in ORDER_OUT]

    def swap_back(back):
        away = call(split_kernel, shape(GROUP, 4, half, DH), *back)
        return back + [lax.ppermute(away, "head", swap)]

    ext_a, *edges_a = gather(0)
    halo_a = halo(*edges_a)
    res_a = interior(ext_a)
    res_a, arrived[1][1] = lax.optimization_barrier((res_a, arrived[1][1]))
    back_a = finish(ext_a, *halo_a, res_a)
    ext_b, *edges_b = gather(1, back_a)
    halo_b = halo(*edges_b)
    res_b = interior(ext_b)
    out_a = give_back(back_a)
    res_b, tied = lax.optimization_barrier((res_b, [out_a[i] for i in (1, 2)]))
    for i, block in zip((1, 2), tied):
        out_a[i] = block
    back_b = finish(ext_b, *halo_b, res_b)
    out_b = give_back(back_b)
    results = [swap_back(out_a), swap_back(out_b)]
    return tuple(unpack(results, half, width))


def solution(mesh):
    placed = P(("blk", "head"), None)
    return jax.shard_map(
        body,
        mesh=mesh,
        in_specs=(placed, placed, placed, placed, P()),
        out_specs=(placed,) * 4,
        check_vma=False,
    )
```
